256 devices in a mesh: tm: 64 (over y, x, z_lo, core), dp: 4 (over z_hi).
Axes of the slice: x: 4, y: 4, z: 8 (z_hi: 4, z_lo: 2; z = z_hi * 2 + z_lo), core: 2. Of those that a mesh axis runs over, the one named last changes fastest.
Arguments:
- resid: bfloat16 [4, 12288, 1536], P('dp', 'tm'), may hold values from -6 to 6
- qkv: bfloat16 [4, 12288, 2304], P('dp', 'tm'), may hold values from -8 to 8
- cotangent: bfloat16 [4, 12288, 1536], P('dp', 'tm'), may hold values from -16 to 16
- lengths: int32 [4], P('dp'), may hold values from 3072 to 12288, as said below
- out_proj: bfloat16 [768, 1536], replicated, may hold values from -0.21875 to 0.21875
- kernel: float32 [31, 1536], replicated, may hold values from -1 to 1
Outputs:
- d_resid: bfloat16 [4, 12288, 1536], P('dp', 'tm')
- d_qkv: bfloat16 [4, 12288, 2304], P('dp', 'tm')
- d_out_proj: float32 [768, 1536], P(None, ('tm', 'dp'))
- d_kernel: float32 [31, 1536], P(None, ('tm', 'dp'))
The draws below stay inside these ranges and needn't reach their ends.
Inputs may be any that keep to these rules, and one draw needn't show every extreme that they name: `lengths`: valid frames come first in each utterance; one utterance has all 12288 frames valid and another a quarter of them.
All inputs are finite; a program needn't handle non-finite values.
Results may differ from the reference program's by a relative error of at most 0.029.
Values may be sent and summed in bfloat16 or wider, within the bound.
A program may use at most 128 MiB of HBM per device.

```python
import jax
import jax.numpy as jnp
from jax import lax

D = 1536
H = 8
HD = 96
KS = 31
TOK = 192
W = 768
FRAMES = 12288
UTT = 4


def draw_qkv(key, part):
    key = jax.random.fold_in(key, 11)
    keys = jax.random.split(key, 1)
    shape = (UTT, FRAMES, 3 * W)
    column = jnp.arange(3 * W)
    col_scale = jnp.where(column < 2 * W, 1.4, 1.0).astype(jnp.float32)
    result = jnp.clip(jax.random.normal(keys[0], shape, jnp.float32) * col_scale, -8.0, 8.0)
    return result.astype(jnp.bfloat16)


def draw_lengths(key, part):
    key = jax.random.fold_in(key, 23)
    keys = jax.random.split(key, 2)
    drawn = jax.random.randint(keys[0], (UTT,), FRAMES // 4, FRAMES + 1)
    order = jax.random.permutation(keys[1], UTT)
    drawn = jnp.where(order == 0, FRAMES, jnp.where(order == 1, FRAMES // 4, drawn))
    return drawn.astype(jnp.int32)


def with_spikes(values, stream_key, source, target, shards_of, factor):
    owner, partner = [(jnp.arange(values.shape[dim]) // (values.shape[dim] // shards_of)).reshape([-1 if axis == dim else 1 for axis in range(values.ndim)]) for dim in (source, target)]
    chosen = jax.random.permutation(stream_key, shards_of)[partner]
    strong = (owner == chosen) | (owner == (partner + shards_of // 2) % shards_of)
    return jnp.where(strong, factor * values, values)


def steps_of(stream_key, extent, shards, least, largest):
    def one(position, blocks):
        steps = jax.random.uniform(jax.random.fold_in(jax.random.fold_in(stream_key, 6), position), (blocks,), jnp.float32, least / len(shards), largest / len(shards))
        return jnp.repeat(jnp.exp(steps), extent[position] // blocks).reshape((-1,) + (1,) * (len(extent) - position - 1))

    factor_of = one(*shards[0])
    for cut in shards[1:]:
        factor_of = factor_of * one(*cut)
    return factor_of


def scatter_about(own_key, extent, width, limit, shards=(), kind=jnp.bfloat16):
    array = width * jax.random.normal(own_key, extent, jnp.float32)
    if shards:
        array = array * steps_of(own_key, extent, shards, -0.22, 0.18)
    return jnp.clip(array, -limit, limit).astype(kind)


def gaussian_with(stream_key, extent, spread, bound, pieces, heavy, held_as=jnp.bfloat16):
    values = spread * jax.random.normal(stream_key, extent, jnp.float32)
    if pieces:
        values = values * steps_of(stream_key, extent, pieces, -0.22, 0.18)
    return jnp.clip(with_spikes(values, jax.random.fold_in(stream_key, 3), *heavy), -bound, bound).astype(held_as)


def setup_inputs(seed: int = 0) -> dict:
    streams_of = jax.random.split(jax.random.key(seed), 7)
    return {
        "resid": scatter_about(streams_of[0], (UTT, FRAMES, D), 1.0, 6.0, ((0, 4), (1, 64))),
        "qkv": draw_qkv(jax.random.fold_in(streams_of[6], 71), 0),
        "cotangent": gaussian_with(streams_of[2], (UTT, FRAMES, D), 1.0, 16.0, ((0, 4), (1, 64)), (1, 2, 64, 4.0)),
        "lengths": draw_lengths(jax.random.fold_in(streams_of[6], 71), 0),
        "out_proj": scatter_about(streams_of[4], (W, D), W ** -0.5, 0.21875),
        "kernel": scatter_about(streams_of[5], (KS, D), KS ** -0.5, 1.0, (), jnp.float32),
    }


NEG_FILL = -1.0e9


def head_scores(q_head, k_head, key_open):
    scores = lax.dot_general(q_head, k_head, (((1,), (1,)), ((), ())), preferred_element_type=jnp.float32)
    return jnp.where(key_open[None, :], scores * (HD ** -0.5), NEG_FILL)


def silu_slope(values):
    sigma = jax.nn.sigmoid(values)
    return sigma * (1.0 + values * (1.0 - sigma))


def attend(queries, key_values, key_open, query_valid):
    attn_width = queries.shape[1]
    results = []
    totals = []
    for head_index in range(H):
        first_col = head_index * HD
        last_col = first_col + HD
        scores = head_scores(queries[:, first_col:last_col], key_values[:, first_col:last_col], key_open)
        row_peak = jnp.max(scores, axis=1, keepdims=True)
        summed = jnp.sum(jnp.exp(scores - row_peak), axis=1, keepdims=True)
        log_total = row_peak + jnp.log(summed)
        weights = jnp.exp(scores - log_total).astype(jnp.bfloat16)
        values_head = key_values[:, attn_width + first_col:attn_width + last_col]
        results.append(jnp.dot(weights, values_head, preferred_element_type=jnp.float32))
        totals.append(log_total)
    attended = (jnp.concatenate(results, axis=1) * query_valid[:, None]).astype(jnp.bfloat16)
    return attended, jnp.concatenate(totals, axis=1)


def grad_heads(queries, key_values, key_open, attended_grad, log_totals, deltas, want_query, want_keys):
    attn_width = queries.shape[1]
    query_cols = []
    key_cols = []
    value_cols = []
    for head_index in range(H):
        first_col = head_index * HD
        last_col = first_col + HD
        q_head = queries[:, first_col:last_col]
        k_head = key_values[:, first_col:last_col]
        v_head = key_values[:, attn_width + first_col:attn_width + last_col]
        grad_head = attended_grad[:, first_col:last_col]
        scores = head_scores(q_head, k_head, key_open)
        weights = jnp.exp(scores - log_totals[:, head_index:head_index + 1])
        slopes = lax.dot_general(grad_head, v_head, (((1,), (1,)), ((), ())), preferred_element_type=jnp.float32)
        dscore = (weights * (slopes - deltas[:, head_index:head_index + 1]) * (HD ** -0.5)).astype(jnp.bfloat16)
        if want_query:
            query_cols.append(jnp.dot(dscore, k_head, preferred_element_type=jnp.float32))
        if want_keys:
            key_cols.append(lax.dot_general(dscore, q_head, (((0,), (0,)), ((), ())), preferred_element_type=jnp.float32))
            value_cols.append(lax.dot_general(weights.astype(jnp.bfloat16), grad_head, (((0,), (0,)), ((), ())), preferred_element_type=jnp.float32))
    query_grad = jnp.concatenate(query_cols, axis=1) if want_query else None
    pair_grad = jnp.concatenate(key_cols + value_cols, axis=1) if want_keys else None
    return query_grad, pair_grad


def block_windows(pairs, blocks):
    pair_width = pairs.shape[1]
    padded = jnp.pad(pairs, ((TOK, TOK), (0, 0)))
    before = padded[:-2 * TOK].reshape(blocks, TOK, pair_width)
    middle = padded[TOK:-TOK].reshape(blocks, TOK, pair_width)
    after = padded[2 * TOK:].reshape(blocks, TOK, pair_width)
    return jnp.concatenate([before, middle, after], axis=1)


def reference(resid, qkv, cotangent, lengths, out_proj, kernel):
    frames = resid.shape[1]
    attn_width = out_proj.shape[0]
    blocks = frames // TOK
    reach = (KS - 1) // 2
    proj_total = jnp.zeros((attn_width, D), jnp.float32)
    kernel_total = jnp.zeros((KS, D), jnp.float32)
    resid_grads = []
    qkv_grads = []
    positions = jnp.arange(frames, dtype=jnp.int32)
    block_starts = jnp.arange(blocks, dtype=jnp.int32) * TOK
    offsets = jnp.arange(3 * TOK, dtype=jnp.int32) - TOK
    for utter in range(UTT):
        utter_length = lengths[utter]
        valid = (positions < utter_length).astype(jnp.float32)
        queries = qkv[utter][:, :attn_width]
        pairs = qkv[utter][:, attn_width:]
        windows = block_windows(pairs, blocks)
        key_pos = block_starts[:, None] + offsets[None, :]
        key_open = (key_pos >= 0) & (key_pos < utter_length)
        query_blocks = queries.reshape(blocks, TOK, attn_width)
        valid_blocks = valid.reshape(blocks, TOK)
        attended, log_totals = lax.map(lambda item: attend(item[0], item[1], item[2], item[3]), (query_blocks, windows, key_open, valid_blocks))
        attended = attended.reshape(frames, attn_width)
        log_totals = log_totals.reshape(frames, H)
        mixed_in = (resid[utter].astype(jnp.float32) + jnp.dot(attended, out_proj, preferred_element_type=jnp.float32)).astype(jnp.bfloat16)
        masked = (mixed_in.astype(jnp.float32) * valid[:, None]).astype(jnp.bfloat16)
        padded_in = jnp.pad(masked, ((reach, reach), (0, 0)))
        conv_out = jnp.zeros((frames, D), jnp.float32)
        for tap_index in range(KS):
            conv_out = conv_out + kernel[tap_index] * padded_in[tap_index:tap_index + frames].astype(jnp.float32)
        cot_here = cotangent[utter].astype(jnp.float32)
        conv_grad = (cot_here * silu_slope(conv_out)).astype(jnp.bfloat16)
        padded_grad = jnp.pad(conv_grad, ((reach, reach), (0, 0)))
        back_conv = jnp.zeros((frames, D), jnp.float32)
        kernel_rows = []
        conv_grad_wide = conv_grad.astype(jnp.float32)
        for tap_index in range(KS):
            back_conv = back_conv + kernel[tap_index] * padded_grad[2 * reach - tap_index:2 * reach - tap_index + frames].astype(jnp.float32)
            kernel_rows.append(jnp.sum(conv_grad_wide * padded_in[tap_index:tap_index + frames].astype(jnp.float32), axis=0))
        kernel_total = kernel_total + jnp.stack(kernel_rows, axis=0)
        resid_grad = (cot_here + valid[:, None] * back_conv).astype(jnp.bfloat16)
        proj_total = proj_total + lax.dot_general(attended, resid_grad, (((0,), (0,)), ((), ())), preferred_element_type=jnp.float32)
        attended_grad = (valid[:, None] * lax.dot_general(resid_grad, out_proj, (((1,), (1,)), ((), ())), preferred_element_type=jnp.float32)).astype(jnp.bfloat16)
        deltas = jnp.sum((attended_grad.astype(jnp.float32) * attended.astype(jnp.float32)).reshape(frames, H, HD), axis=2)
        query_grad, parts = lax.map(
            lambda item: grad_heads(item[0], item[1], item[2], item[3], item[4], item[5], True, True),
            (query_blocks, windows, key_open, attended_grad.reshape(blocks, TOK, attn_width), log_totals.reshape(blocks, TOK, H), deltas.reshape(blocks, TOK, H)))
        middle = parts[:, TOK:2 * TOK]
        from_prev = jnp.pad(parts[:-1, 2 * TOK:], ((1, 0), (0, 0), (0, 0)))
        from_next = jnp.pad(parts[1:, :TOK], ((0, 1), (0, 0), (0, 0)))
        pair_grad = (middle + from_prev + from_next).reshape(frames, 2 * attn_width)
        qkv_grads.append(jnp.concatenate([query_grad.reshape(frames, attn_width).astype(jnp.bfloat16), pair_grad.astype(jnp.bfloat16)], axis=1))
        resid_grads.append(resid_grad)
    return jnp.stack(resid_grads, axis=0), jnp.stack(qkv_grads, axis=0), proj_total, kernel_total
```

```python
import jax
import jax.numpy as jnp
from jax import lax
from jax.experimental import pallas as pl
from jax.experimental.pallas import tpu as pltpu
from jax.sharding import PartitionSpec as P

H = 8
HD = 96
T = 192
D = 1536
W = 768
TAPS = 31
CHUNKS = D // 128
EXT = T + 32
RW = W + 128
GROUP = 4 * HD
WINDOWS = ((0, 128), (0, 256), (128, 256), (256, 128))
NEG_FILL = -1000000000.0
SCALE = HD ** (-0.5)
LOG2E = 1.4426950408889634
MESH = pl.DeviceIdType.MESH
F32 = jnp.float32
BF16 = jnp.bfloat16


def dot(a, b, ca, cb):
    return lax.dot_general(a, b, (((ca,), (cb,)), ((), ())), preferred_element_type=F32)


def window_mask(i):
    start, width = WINDOWS[i]
    lane = lax.broadcasted_iota(jnp.int32, (1, width), 1) + start
    return ((lane >= i * HD) & (lane < (i + 1) * HD)).astype(F32)


def join_heads(parts):
    lane = lax.broadcasted_iota(jnp.int32, (1, 128), 1)
    first = jnp.where(lane < 96, parts[0], parts[1][:, :128])
    second = jnp.where(lane < 64, parts[1][:, 128:], parts[2][:, :128])
    third = jnp.where(lane < 32, parts[2][:, 128:], parts[3])
    return jnp.concatenate([first, second, third], axis=1)


def lanes(c, width):
    return pl.ds(pl.multiple_of(c * width, width), width)


def kernel(
    resid_h, qkv_h, cot_h, len_s, proj_h, ker_h,
    dres_h, dqkv_h, dproj_o, dker_o,
    q_v, kv, res_v, cot_v, w_v, ker_v, probs, att_v, g_v, mext, gext, dres_v, out_v, mid,
    hs, hm, gs, hg, kt, pt, s_a, r_a, s_1, r_1, k_1, s_2, r_2, k_2, s_3, r_3,
    d_left, d_right, from_left, from_right,
    loc_sem, nb_send, nb_recv, rs_send, rs_recv,
):
    tm = lax.axis_index("tm")
    zh = lax.axis_index("dp")
    core = tm % 2
    zl = (tm // 2) % 2
    x = (tm // 4) % 4
    y = tm // 16
    other = 1 - core
    zz = zh * 2 + zl

    def device(y_, x_, zl_, core_, zh_):
        return {"tm": ((y_ * 4 + x_) * 2 + zl_) * 2 + core_, "dp": zh_}

    left = {"tm": (tm + 63) % 64, "dp": zh}
    right = {"tm": (tm + 1) % 64, "dp": zh}
    mate = device(y, x, zl, other, zh)
    first_peers = [device((y + e * other) % 4, (x + e * core) % 4, zl, core, zh) for e in (1, 2, 3)]
    second_peers = [device((y + e * core) % 4, (x + e * other) % 4, zl, core, zh) for e in (1, 2, 3)]
    z_peers = []
    for e in range(1, 8):
        z_to = (zz + e) % 8
        z_peers.append((device(y, x, z_to % 2, core, z_to // 2), (z_to % 2) * 4 + z_to // 2))

    def local(src, dst, i):
        return pltpu.make_async_copy(src, dst, loc_sem.at[i])

    def near(src, dst, i, to):
        return pltpu.make_async_remote_copy(
            src_ref=src, dst_ref=dst, send_sem=nb_send.at[i], recv_sem=nb_recv.at[i],
            device_id=to, device_id_type=MESH,
        )

    def far(src, dst, i, to):
        return pltpu.make_async_remote_copy(
            src_ref=src, dst_ref=dst, send_sem=rs_send.at[i], recv_sem=rs_recv.at[i],
            device_id=to, device_id_type=MESH,
        )

    ins = [
        local(qkv_h.at[0, :, 0:W], q_v, 0),
        local(qkv_h.at[0, :, W : 3 * W], kv.at[T : 2 * T], 1),
        local(proj_h, w_v, 2),
        local(resid_h.at[0], res_v, 3),
        local(cot_h.at[0], cot_v, 4),
        local(ker_h, ker_v, 5),
    ]
    for copy in ins:
        copy.start()

    barrier = pltpu.get_barrier_semaphore()
    everyone = [left, right] + first_peers + second_peers + [peer for peer, _ in z_peers]
    for peer in everyone:
        pl.semaphore_signal(barrier, inc=1, device_id=peer, device_id_type=MESH)
    pl.semaphore_wait(barrier, len(everyone))

    kv_copies = [
        near(qkv_h.at[0, :, W : 3 * W], kv.at[0:T], 0, right),
        near(qkv_h.at[0, :, W : 3 * W], kv.at[2 * T : 3 * T], 1, left),
    ]
    for copy in kv_copies:
        copy.start()

    length = len_s[0]
    first_frame = tm * T
    frame = first_frame + lax.broadcasted_iota(jnp.int32, (T, 1), 0)
    valid = (frame < length).astype(F32)
    key = first_frame - T + lax.broadcasted_iota(jnp.int32, (1, 3 * T), 1)
    key_open = (key >= 0) & (key < length)
    has_left = (tm > 0).astype(F32)
    has_right = (tm < 63).astype(F32)

    for copy in ins:
        copy.wait()
    for copy in kv_copies:
        copy.wait()

    def forward_group(group):
        base = group * GROUP
        outs = []
        for i in range(4):
            start, width = WINDOWS[i]
            cols = slice(base + start, base + start + width)
            v_cols = slice(W + base + start, W + base + start + width)
            q_head = q_v[:, cols] * window_mask(i).astype(BF16)
            scores = dot(q_head, kv[:, cols], 1, 1)
            scores = jnp.where(key_open, scores * (SCALE * LOG2E), NEG_FILL)
            peak = jnp.max(scores, axis=1, keepdims=True)
            weights = jnp.exp2(scores - peak)
            total = jnp.sum(weights, axis=1, keepdims=True)
            weights = (weights * (1.0 / total)).astype(BF16)
            probs[group * 4 + i] = weights
            outs.append(dot(weights, kv[:, v_cols], 1, 0))
        att_v[:, base : base + GROUP] = (join_heads(outs) * valid).astype(BF16)

    forward_group(0)
    forward_group(1)

    def project(j, carry):
        cols = lanes(j, 256)
        mixed = res_v[:, cols].astype(F32) + dot(att_v[...], w_v[:, cols], 1, 0)
        masked = (mixed.astype(BF16).astype(F32) * valid).astype(BF16)
        hs[0, :, cols] = masked[0:16]
        hs[1, :, cols] = masked[T - 16 : T]
        wide = masked.astype(F32)
        mext[2 * j, 16 : 16 + T, :] = wide[:, :128]
        mext[2 * j + 1, 16 : 16 + T, :] = wide[:, 128:]
        return carry

    lax.fori_loop(0, D // 256, project, 0)
    mask_halo = [near(hs.at[0], hm.at[1], 2, left), near(hs.at[1], hm.at[0], 3, right)]
    for copy in mask_halo:
        copy.start()

    def taps_of(c, flip):
        cols = lanes(c, 128)
        order = range(TAPS - 1, -1, -1) if flip else range(TAPS)
        return [ker_v[j : j + 1, cols] for j in order]

    def convolve(src, taps, c, row, count):
        total = taps[0] * src[c, row + 1 : row + 1 + count, :]
        for j in range(1, TAPS):
            total = total + taps[j] * src[c, row + 1 + j : row + 1 + j + count, :]
        return total

    def conv_rows(c, row, count):
        conv = convolve(mext, taps_of(c, False), c, row, count)
        sigma = jax.nn.sigmoid(conv)
        slope = sigma * (1.0 + conv * (1.0 - sigma))
        grad = (cot_v[row : row + count, lanes(c, 128)].astype(F32) * slope).astype(BF16)
        gext[c, 16 + row : 16 + row + count, :] = grad.astype(F32)
        return grad

    def back_rows(c, row, count):
        back = convolve(gext, taps_of(c, True), c, row, count)
        cot = cot_v[row : row + count, lanes(c, 128)].astype(F32)
        dres_v[row : row + count, lanes(c, 128)] = (
            cot + valid[row : row + count] * back
        ).astype(BF16)

    def conv_inner(c, carry):
        conv_rows(c, 16, 80)
        conv_rows(c, 96, 80)
        return carry

    lax.fori_loop(0, CHUNKS, conv_inner, 0)
    for copy in mask_halo:
        copy.wait()

    def conv_edge(c, carry):
        cols = lanes(c, 128)
        mext[c, 0:16, :] = hm[0, :, cols].astype(F32) * has_left
        mext[c, 16 + T : 32 + T, :] = hm[1, :, cols].astype(F32) * has_right
        gs[0, :, cols] = conv_rows(c, 0, 16)
        gs[1, :, cols] = conv_rows(c, T - 16, 16)
        return carry

    lax.fori_loop(0, CHUNKS, conv_edge, 0)
    grad_halo = [near(gs.at[0], hg.at[1], 4, left), near(gs.at[1], hg.at[0], 5, right)]
    for copy in grad_halo:
        copy.start()

    kt[...] = jnp.zeros_like(kt)

    def back_inner(c, carry):
        grad = gext[c, 16 : 16 + T, :]
        for j in range(TAPS):
            term = grad * mext[c, 1 + j : 1 + j + T, :]
            kt[j : j + 1, :] = jnp.sum(term, axis=0, keepdims=True)
        pt[lanes(c, 128), W:RW] = kt[...].T
        back_rows(c, 16, 80)
        back_rows(c, 96, 80)
        return carry

    lax.fori_loop(0, CHUNKS, back_inner, 0)
    for copy in grad_halo:
        copy.wait()

    def back_edge(c, carry):
        cols = lanes(c, 128)
        gext[c, 0:16, :] = hg[0, :, cols].astype(F32) * has_left
        gext[c, 16 + T : 32 + T, :] = hg[1, :, cols].astype(F32) * has_right
        back_rows(c, 0, 16)
        back_rows(c, T - 16, 16)
        return carry

    lax.fori_loop(0, CHUNKS, back_edge, 0)
    out_resid = local(dres_v, dres_h.at[0], 6)
    out_resid.start()

    def project_grad(j, carry):
        cols = lanes(j, 384)
        pt[cols, 0:W] = dot(dres_v[:, cols], att_v[...], 0, 0)
        return carry

    lax.fori_loop(0, 4, project_grad, 0)

    place, second = y * other + x * core, x * other + y * core

    def own_rows(a, b, which):
        y_, x_ = a * (1 - which) + b * which, b * (1 - which) + a * which
        row = (y_ * 4 + x_) * 96 + which * 24
        return jnp.concatenate(
            [
                pt[pl.ds(pl.multiple_of(row, 8), 24), :],
                pt[pl.ds(pl.multiple_of(row + 48, 8), 24), :],
            ],
            axis=0,
        )

    mate_copies = []
    for s in range(4):
        for b in range(4):
            s_a[s, b] = own_rows((second + 1 + s) % 4, b, other).astype(BF16)
        mate_copies.append(far(s_a.at[s], r_a.at[s], s, mate))
        mate_copies[-1].start()

    def attended_grad(j, carry):
        cols = lanes(j, 256)
        g_v[:, cols] = (valid * dot(dres_v[...], w_v[cols, :], 1, 1)).astype(BF16)
        return carry

    lax.fori_loop(0, W // 256, attended_grad, 0)

    def backward_group(group):
        base = group * GROUP
        d_q, d_k, d_v = [], [], []
        for i in range(4):
            start, width = WINDOWS[i]
            cols = slice(base + start, base + start + width)
            v_cols = slice(W + base + start, W + base + start + width)
            g_win = g_v[:, cols]
            g_head = g_win * window_mask(i).astype(BF16)
            delta = jnp.sum(
                g_head.astype(F32) * att_v[:, cols].astype(F32), axis=1, keepdims=True
            )
            slopes = dot(g_head, kv[:, v_cols], 1, 1)
            weights = probs[group * 4 + i]
            dscore = (weights.astype(F32) * ((slopes - delta) * SCALE)).astype(BF16)
            d_q.append(dot(dscore, kv[:, cols], 1, 0))
            d_k.append(dot(dscore, q_v[:, cols], 0, 0))
            d_v.append(dot(weights, g_win, 0, 0))
        out_v[:, base : base + GROUP] = join_heads(d_q).astype(BF16)
        for part, grads in enumerate((d_k, d_v)):
            whole = join_heads(grads)
            cols = slice(part * GROUP, (part + 1) * GROUP)
            d_left[group, :, cols] = whole[0:T].astype(BF16)
            mid[group, :, cols] = whole[T : 2 * T]
            d_right[group, :, cols] = whole[2 * T : 3 * T].astype(BF16)
        copies = [
            near(d_left.at[group], from_right.at[group], 6 + 2 * group, left),
            near(d_right.at[group], from_left.at[group], 7 + 2 * group, right),
        ]
        for copy in copies:
            copy.start()
        return copies

    first_copies = []
    for s in range(4):
        a = (place + 1 + s) % 4
        mate_copies[s].wait()
        for b in range(4):
            total = own_rows(a, b, core) + r_a[s, b].astype(F32)
            if s < 3:
                s_1[s, b] = total.astype(BF16)
            else:
                k_1[b] = total
        if s < 3:
            first_copies.append(far(s_1.at[s], r_1.at[s], 4 + s, first_peers[s]))
            first_copies[-1].start()

    pair_copies = backward_group(0)

    for copy in first_copies:
        copy.wait()
    second_copies = []
    for s in range(4):
        b = (second + 1 + s) % 4
        total = k_1[b]
        for e in range(3):
            total = total + r_1[e, b].astype(F32)
        if s < 3:
            s_2[s] = total.astype(BF16)
            second_copies.append(far(s_2.at[s], r_2.at[s], 7 + s, second_peers[s]))
            second_copies[-1].start()
        else:
            k_2[...] = total

    pair_copies += backward_group(1)

    for copy in second_copies:
        copy.wait()
    total = k_2[...]
    for e in range(3):
        total = total + r_2[e].astype(F32)
    s_3[...] = jnp.zeros_like(s_3)
    for part in range(8):
        s_3[part, 0:6, :] = total[part * 6 : part * 6 + 6]
    z_copies = []
    for e, (peer, part) in enumerate(z_peers):
        z_copies.append(far(s_3.at[part], r_3.at[e], 10 + e, peer))
        z_copies[-1].start()

    for copy in pair_copies:
        copy.wait()
    for group in range(2):
        for part in range(2):
            cols = slice(part * GROUP, (part + 1) * GROUP)
            whole = (
                mid[group, :, cols]
                + from_left[group, :, cols].astype(F32)
                + from_right[group, :, cols].astype(F32)
            )
            start = (1 + part) * W + group * GROUP
            out_v[:, start : start + GROUP] = whole.astype(BF16)
    out_qkv = local(out_v, dqkv_h.at[0], 7)
    out_qkv.start()

    for copy in z_copies:
        copy.wait()
    total = s_3[zl * 4 + zh]
    for e in range(7):
        total = total + r_3[e]
    turned = jnp.concatenate([total, jnp.zeros((120, RW), F32)], axis=0).T
    dproj_o[...] = turned[0:W, 0:6]
    dker_o[...] = turned[W : W + TAPS, 0:6]
    out_resid.wait()
    out_qkv.wait()


def local(resid, qkv, cotangent, lengths, out_proj, ker):
    hbm = pl.BlockSpec(memory_space=pl.ANY)
    vmem = pl.BlockSpec(memory_space=pltpu.VMEM)
    scratch = [
        ((T, W), BF16), ((3 * T, 2 * W), BF16), ((T, D), BF16), ((T, D), BF16),
        ((W, D), BF16), ((TAPS, D), F32), ((H, T, 3 * T), BF16), ((T, W), BF16),
        ((T, W), BF16), ((CHUNKS, EXT, 128), F32), ((CHUNKS, EXT, 128), F32), ((T, D), BF16),
        ((T, 3 * W), BF16), ((2, T, 2 * GROUP), F32),
        ((2, 16, D), BF16), ((2, 16, D), BF16), ((2, 16, D), BF16), ((2, 16, D), BF16),
        ((128, 128), F32), ((D, RW), F32),
        ((4, 4, 48, RW), BF16), ((4, 4, 48, RW), BF16),
        ((3, 4, 48, RW), BF16), ((3, 4, 48, RW), BF16), ((4, 48, RW), F32),
        ((3, 48, RW), BF16), ((3, 48, RW), BF16), ((48, RW), F32),
        ((8, 8, RW), F32), ((7, 8, RW), F32),
        ((2, T, 2 * GROUP), BF16), ((2, T, 2 * GROUP), BF16),
        ((2, T, 2 * GROUP), BF16), ((2, T, 2 * GROUP), BF16),
    ]
    return pl.pallas_call(
        kernel,
        out_shape=[
            jax.ShapeDtypeStruct((1, T, D), BF16),
            jax.ShapeDtypeStruct((1, T, 3 * W), BF16),
            jax.ShapeDtypeStruct((W, 6), F32),
            jax.ShapeDtypeStruct((TAPS, 6), F32),
        ],
        in_specs=[hbm, hbm, hbm, pl.BlockSpec(memory_space=pltpu.SMEM), hbm, hbm],
        out_specs=[hbm, hbm, vmem, vmem],
        scratch_shapes=[pltpu.VMEM(shape, kind) for shape, kind in scratch]
        + [
            pltpu.SemaphoreType.DMA((8,)),
            pltpu.SemaphoreType.DMA((10,)),
            pltpu.SemaphoreType.DMA((10,)),
            pltpu.SemaphoreType.DMA((17,)),
            pltpu.SemaphoreType.DMA((17,)),
        ],
        compiler_params=pltpu.CompilerParams(
            collective_id=0, has_side_effects=True, vmem_limit_bytes=56 * 2**20
        ),
        cost_estimate=pl.CostEstimate(
            flops=3_000_000_000, bytes_accessed=8_000_000, transcendentals=1_000_000
        ),
    )(resid, qkv, cotangent, lengths, out_proj, ker)


def solution(mesh):
    in_specs = (P("dp", "tm", None), P("dp", "tm", None), P("dp", "tm", None), P("dp"), P(), P())
    out_specs = (
        P("dp", "tm", None),
        P("dp", "tm", None),
        P(None, ("tm", "dp")),
        P(None, ("tm", "dp")),
    )
    return jax.shard_map(local, mesh=mesh, in_specs=in_specs, out_specs=out_specs, check_vma=False)
```

```python
import jax
import jax.numpy as jnp
from jax import lax
from jax.experimental import pallas as pl
from jax.experimental.pallas import tpu as pltpu
from jax.sharding import PartitionSpec as P

H = 8
HD = 96
T = 192
D = 1536
W = 768
TAPS = 31
CHUNKS = D // 128
EDGE = 16
REACH = 2 * EDGE
RW = W + 128
KEYS = 3 * T
GROUP = 4 * HD
WINDOWS = ((0, 128), (0, 256), (128, 256), (256, 128))
NEG_FILL = -1000000000.0
SCALE = HD ** (-0.5)
LOG2E = 1.4426950408889634
MESH = pl.DeviceIdType.MESH
F32 = jnp.float32
BF16 = jnp.bfloat16


def dot(a, b, ca, cb):
    return lax.dot_general(a, b, (((ca,), (cb,)), ((), ())), preferred_element_type=F32)


def window_mask(i):
    start, width = WINDOWS[i]
    lane = lax.broadcasted_iota(jnp.int32, (1, width), 1) + start
    return ((lane >= i * HD) & (lane < (i + 1) * HD)).astype(F32)


def join_heads(parts):
    lane = lax.broadcasted_iota(jnp.int32, (1, 128), 1)
    first = jnp.where(lane < 96, parts[0], parts[1][:, :128])
    second = jnp.where(lane < 64, parts[1][:, 128:], parts[2][:, :128])
    third = jnp.where(lane < 32, parts[2][:, 128:], parts[3])
    return jnp.concatenate([first, second, third], axis=1)


def lanes(c, width):
    return pl.ds(pl.multiple_of(c * width, width), width)


def kernel(
    resid_h, qkv_h, cot_h, len_s, proj_h, ker_h,
    dres_h, dqkv_h, sums_o,
    q_all, kv, res_v, cot_v, w_v, ker_v, probs, probs_k, stat, att_v, att_m, go,
    mext, gext, dres_v, out_v, hs, hm, hc, kt, kt_part, kt_all, turned, lhs_own, lhs_out, lhs_in,
    s_2hop, r_2hop, s_up, s_down, keep_up, keep_down, r_up, r_down, own_1,
    s_2, r_2, own_2, s_3, r_3,
    loc_sem, nb_send, nb_recv, rs_send, rs_recv,
):
    tm = lax.axis_index("tm")
    zh = lax.axis_index("dp")
    core = tm % 2
    zl = (tm // 2) % 2
    x = (tm // 4) % 4
    y = tm // 16
    other = 1 - core
    zz = zh * 2 + zl

    def device(y_, x_, zl_, core_, zh_):
        return {"tm": ((y_ * 4 + x_) * 2 + zl_) * 2 + core_, "dp": zh_}

    left = {"tm": (tm + 63) % 64, "dp": zh}
    right = {"tm": (tm + 1) % 64, "dp": zh}
    mate = device(y, x, zl, other, zh)
    up = device((y + other) % 4, (x + core) % 4, zl, core, zh)
    down = device((y + 3 * other) % 4, (x + 3 * core) % 4, zl, core, zh)
    second_peers = [device((y + e * core) % 4, (x + e * other) % 4, zl, core, zh) for e in (1, 2, 3)]
    z_peers = []
    for e in range(1, 8):
        z_to = (zz + e) % 8
        z_peers.append((device(y, x, z_to % 2, core, z_to // 2), (z_to % 2) * 4 + z_to // 2))

    def local(src, dst, i):
        return pltpu.make_async_copy(src, dst, loc_sem.at[i])

    def near(src, dst, i, to):
        return pltpu.make_async_remote_copy(
            src_ref=src, dst_ref=dst, send_sem=nb_send.at[i], recv_sem=nb_recv.at[i],
            device_id=to, device_id_type=MESH,
        )

    def far(src, dst, i, to):
        return pltpu.make_async_remote_copy(
            src_ref=src, dst_ref=dst, send_sem=rs_send.at[i], recv_sem=rs_recv.at[i],
            device_id=to, device_id_type=MESH,
        )

    def start(copies):
        for copy in copies:
            copy.start()
        return copies

    def wait(copies):
        for copy in copies:
            copy.wait()

    low, own, high = slice(0, T), slice(T, 2 * T), slice(2 * T, 3 * T)

    ins = start([
        local(qkv_h.at[0, :, 0:W], q_all.at[own], 0),
        local(qkv_h.at[0, :, W : 3 * W], kv.at[own], 1),
        local(proj_h, w_v, 2),
        local(resid_h.at[0], res_v, 3),
        local(cot_h.at[0], cot_v, 4),
        local(ker_h, ker_v, 5),
    ])

    barrier = pltpu.get_barrier_semaphore()
    everyone = [left, right, up, down] + second_peers + [peer for peer, _ in z_peers]
    for peer in everyone:
        pl.semaphore_signal(barrier, inc=1, device_id=peer, device_id_type=MESH)
    pl.semaphore_wait(barrier, len(everyone))

    kv_copies = []
    for group in range(2):
        for part in range(2):
            cols = slice(part * W + group * GROUP, part * W + (group + 1) * GROUP)
            src = qkv_h.at[0, :, W + cols.start : W + cols.stop]
            i = group * 4 + part * 2
            kv_copies.append(near(src, kv.at[low, cols], i, right))
            kv_copies.append(near(src, kv.at[high, cols], i + 1, left))
    start(kv_copies)

    length = len_s[0]
    first_frame = tm * T
    frame = first_frame + lax.broadcasted_iota(jnp.int32, (T, 1), 0)
    valid = (frame < length).astype(F32)
    key = first_frame - T + lax.broadcasted_iota(jnp.int32, (1, KEYS), 1)
    key_open = (key >= 0) & (key < length)
    own_key = first_frame + lax.broadcasted_iota(jnp.int32, (1, T), 1)
    near_query = first_frame - T + lax.broadcasted_iota(jnp.int32, (KEYS, 1), 0)
    pair_open = (own_key < length) & (near_query >= 0) & (near_query < 64 * T)
    has_left = (tm > 0).astype(F32)
    has_right = (tm < 63).astype(F32)
    lane = lax.broadcasted_iota(jnp.int32, (1, 128), 1)

    kt[...] = jnp.zeros_like(kt)
    att_v[T:256, :] = jnp.zeros((256 - T, W), BF16)
    s_3[...] = jnp.zeros_like(s_3)

    wait(ins)
    wait(kv_copies[:4])

    def forward_group(group, stats):
        base = group * GROUP
        outs = []
        for i in range(4):
            start_, width = WINDOWS[i]
            cols = slice(base + start_, base + start_ + width)
            v_cols = slice(W + base + start_, W + base + start_ + width)
            q_head = q_all[own, cols] * window_mask(i).astype(BF16)
            scores = dot(q_head, kv[:, cols], 1, 1)
            scores = jnp.where(key_open, scores * (SCALE * LOG2E), NEG_FILL)
            peak = jnp.max(scores, axis=1, keepdims=True)
            weights = jnp.exp2(scores - peak)
            total = jnp.sum(weights, axis=1, keepdims=True)
            weights = (weights * (1.0 / total)).astype(BF16)
            probs[group * 4 + i] = weights
            stats = jnp.where(lane == group * 4 + i, peak + jnp.log2(total), stats)
            outs.append(dot(weights, kv[:, v_cols], 1, 0))
        att_v[0:T, base : base + GROUP] = (join_heads(outs) * valid).astype(BF16)
        return stats

    stats = forward_group(0, jnp.zeros((T, 128), F32))
    wait(kv_copies[4:])
    early = start([
        near(cot_v.at[0:EDGE], hc.at[1], 8, left),
        near(cot_v.at[T - EDGE : T], hc.at[0], 9, right),
    ])
    q_copies = start([
        near(q_all.at[own, 0:GROUP], q_all.at[low, 0:GROUP], 10, right),
        near(q_all.at[own, 0:GROUP], q_all.at[high, 0:GROUP], 11, left),
    ])
    stat[own, :] = forward_group(1, stats)
    early += start([far(att_v, att_m, 0, mate)])

    def project(j, carry):
        cols = lanes(j, 256)
        mixed = res_v[:, cols].astype(F32) + dot(att_v[0:T, :], w_v[:, cols], 1, 0)
        masked = (mixed.astype(BF16).astype(F32) * valid).astype(BF16)
        hs[0, :, cols] = masked[0:REACH]
        hs[1, :, cols] = masked[T - REACH : T]
        wide = masked.astype(F32)
        mext[2 * j, REACH : REACH + T, :] = wide[:, :128]
        mext[2 * j + 1, REACH : REACH + T, :] = wide[:, 128:]
        return carry

    lax.fori_loop(0, D // 256, project, 0)
    mask_halo = start([near(hs.at[0], hm.at[1], 12, left), near(hs.at[1], hm.at[0], 13, right)])

    def windows(src, c, first, count):
        for s in range(8):
            taps = range(s, TAPS, 8)
            window = src[c, first + s : first + s + count + 8 * (len(taps) - 1), :]
            for place, j in enumerate(taps):
                yield j, window[8 * place : 8 * place + count]

    def convolve(src, c, first, count, flip):
        total = None
        for j, rows in windows(src, c, first, count):
            tap = TAPS - 1 - j if flip else j
            term = ker_v[tap : tap + 1, lanes(c, 128)] * rows
            total = term if total is None else total + term
        return total

    def conv_rows(c, row, count, cot):
        conv = convolve(mext, c, row + REACH - 15, count, False)
        sigma = jax.nn.sigmoid(conv)
        slope = sigma * (1.0 + conv * (1.0 - sigma))
        grad = (cot * slope).astype(BF16).astype(F32)
        gext[c, EDGE + row : EDGE + row + count, :] = grad

    def back_rows(c, row, count):
        cols = lanes(c, 128)
        back = convolve(gext, c, row + EDGE - 15, count, True)
        cot = cot_v[row : row + count, cols].astype(F32)
        dres_v[row : row + count, cols] = (cot + valid[row : row + count] * back).astype(BF16)

    def kernel_terms(c, row, count, sums):
        grad = gext[c, EDGE + row : EDGE + row + count, :]
        for j, rows in windows(mext, c, row + REACH - 15, count):
            term = jnp.sum((grad * rows).reshape(count // 8, 8, 128), axis=0)
            sums[j] = term if sums[j] is None else sums[j] + term

    def conv_inner(c, carry):
        for row in (16, 96):
            conv_rows(c, row, 80, cot_v[row : row + 80, lanes(c, 128)].astype(F32))
        sums = [None] * TAPS
        for row in (16, 96):
            kernel_terms(c, row, 80, sums)
        for j in range(TAPS):
            kt_part[c, 8 * j : 8 * j + 8, :] = sums[j]
        return carry

    lax.fori_loop(0, CHUNKS // 2, conv_inner, 0)
    q_copies += start([
        near(q_all.at[own, GROUP:W], q_all.at[low, GROUP:W], 14, right),
        near(q_all.at[own, GROUP:W], q_all.at[high, GROUP:W], 15, left),
        near(stat.at[own], stat.at[low], 16, right),
        near(stat.at[own], stat.at[high], 17, left),
    ])
    lax.fori_loop(CHUNKS // 2, CHUNKS, conv_inner, 0)
    wait(early)
    wait(mask_halo)

    def edges_and_back(c, carry):
        cols = lanes(c, 128)
        mext[c, 0:REACH, :] = hm[0, :, cols].astype(F32) * has_left
        mext[c, REACH + T : 2 * REACH + T, :] = hm[1, :, cols].astype(F32) * has_right
        cot = cot_v[0:EDGE, cols].astype(F32)
        before = hc[0, :, cols].astype(F32) * has_left
        conv_rows(c, -EDGE, REACH, jnp.concatenate([before, cot], axis=0))
        cot = cot_v[T - EDGE : T, cols].astype(F32)
        after = hc[1, :, cols].astype(F32) * has_right
        conv_rows(c, T - EDGE, REACH, jnp.concatenate([cot, after], axis=0))
        sums = [kt_part[c, 8 * j : 8 * j + 8, :] for j in range(TAPS)]
        kernel_terms(c, 0, EDGE, sums)
        kernel_terms(c, T - EDGE, EDGE, sums)
        for j in range(TAPS):
            kt[j : j + 1, :] = jnp.sum(sums[j], axis=0, keepdims=True)
        kt_all[cols, :] = kt[...].T
        back_rows(c, 0, 96)
        back_rows(c, 96, 96)
        grad = dres_v[:, cols].astype(F32)
        turned[cols, :] = jnp.concatenate([grad, jnp.zeros((256 - T, 128), F32)], axis=0).T
        return carry

    def rows_of(ref, block, which):
        row = block * 96 + which * 24
        return jnp.concatenate(
            [
                ref[pl.ds(pl.multiple_of(row, 8), 24), :],
                ref[pl.ds(pl.multiple_of(row + 48, 8), 24), :],
            ],
            axis=0,
        )

    pair_copies = []
    for quarter in range(4):
        lax.fori_loop(3 * quarter, 3 * quarter + 3, edges_and_back, 0)
        for block in range(4 * quarter, 4 * quarter + 4):
            lhs_out[block, :, 0:256] = rows_of(turned, block, other).astype(BF16)
            lhs_out[block, :, 256:384] = rows_of(kt_all, block, other).astype(BF16)
        quarters = slice(4 * quarter, 4 * quarter + 4)
        pair_copies += start([far(lhs_out.at[quarters], lhs_in.at[quarters], 15 + quarter, mate)])
    out_resid = start([local(dres_v, dres_h.at[0], 6)])

    place, second = y * other + x * core, x * other + y * core

    def attended_grad(j, carry):
        go[own, pl.ds(pl.multiple_of(128 + j * 256, 128), 256)] = (
            valid * dot(dres_v[...], w_v[lanes(j, 256), :], 1, 1)
        ).astype(BF16)
        return carry

    lax.fori_loop(0, W // 256, attended_grad, 0)
    deltas = jnp.zeros((T, 128), F32)
    for head in range(H):
        start_, width = WINDOWS[head % 4]
        first = head // 4 * GROUP + start_
        product = (
            go[own, 128 + first : 128 + first + width].astype(F32)
            * att_v[0:T, first : first + width].astype(F32)
        )
        delta = jnp.sum(product * window_mask(head % 4), axis=1, keepdims=True)
        coarse = delta.astype(BF16).astype(F32)
        deltas = jnp.where(lane == head, coarse, deltas)
        deltas = jnp.where(lane == H + head, delta - coarse, deltas)
    go[own, 0:128] = deltas.astype(BF16)
    first, last = slice(0, 128 + GROUP), slice(128 + GROUP, 128 + W)

    def send_grads(cols, i):
        return start([
            near(go.at[own, cols], go.at[low, cols], i, right),
            near(go.at[own, cols], go.at[high, cols], i + 1, left),
        ])

    grad_copies = [send_grads(first, 18)]

    def gather_own(block, carry):
        lhs_own[block] = rows_of(turned, block, core).astype(BF16)
        return carry

    lax.fori_loop(0, 16, gather_own, 0)
    wait(pair_copies)

    def pair_sum(a):
        blocks = [(a * other + b * core) * 4 + b * other + a * core for b in range(4)]
        mine = jnp.concatenate([lhs_own[block] for block in blocks], axis=0)
        theirs = jnp.concatenate([lhs_in[block, :, 0:256] for block in blocks], axis=0)
        main = dot(mine, att_v[...], 1, 0) + dot(theirs, att_m[...], 1, 0)
        side = jnp.concatenate(
            [
                rows_of(kt_all, block, core) + lhs_in[block, :, 256:384].astype(F32)
                for block in blocks
            ],
            axis=0,
        )
        return jnp.concatenate([main, side], axis=1)

    half = 96
    whole = pair_sum((place + 2) % 4)
    s_2hop[0:half] = whole[0:half].astype(BF16)
    s_2hop[half:T] = whole[half:T].astype(BF16)
    two_hop = start([
        far(s_2hop.at[0:half], r_2hop.at[0:half], 1, up),
        far(s_2hop.at[half:T], r_2hop.at[half:T], 2, down),
    ])
    whole = pair_sum((place + 1) % 4)
    keep_up[...] = whole[0:half]
    s_up[half:T] = whole[half:T].astype(BF16)
    one_hop = start([far(s_up.at[half:T], r_up.at[half:T], 3, up)])
    whole = pair_sum((place + 3) % 4)
    s_down[0:half] = whole[0:half].astype(BF16)
    keep_down[...] = whole[half:T]
    one_hop += start([far(s_down.at[0:half], r_down.at[0:half], 4, down)])
    own_1[...] = pair_sum(place)

    def query_group(group):
        base = group * GROUP
        d_q = []
        for i in range(4):
            head = group * 4 + i
            start_, width = WINDOWS[i]
            cols = slice(base + start_, base + start_ + width)
            v_cols = slice(W + base + start_, W + base + start_ + width)
            g_cols = slice(128 + base + start_, 128 + base + start_ + width)
            g_head = go[own, g_cols] * window_mask(i).astype(BF16)
            delta = go[own, head : head + 1].astype(F32) + go[own, H + head : H + head + 1].astype(F32)
            slopes = dot(g_head, kv[:, v_cols], 1, 1)
            dscore = (probs[head].astype(F32) * ((slopes - delta) * SCALE)).astype(BF16)
            d_q.append(dot(dscore, kv[:, cols], 1, 0))
        out_v[:, base : base + GROUP] = join_heads(d_q).astype(BF16)

    def probs_group(group):
        base = group * GROUP
        for i in range(4):
            head = group * 4 + i
            start_, width = WINDOWS[i]
            cols = slice(base + start_, base + start_ + width)
            k_head = kv[own, cols] * window_mask(i).astype(BF16)
            scores = dot(q_all[:, cols], k_head, 1, 1)
            scores = jnp.where(pair_open, scores * (SCALE * LOG2E), NEG_FILL)
            probs_k[head] = jnp.exp2(scores - stat[:, head : head + 1]).astype(BF16)

    def key_group(group):
        base = group * GROUP
        d_k, d_v = [], []
        for i in range(4):
            head = group * 4 + i
            start_, width = WINDOWS[i]
            cols = slice(base + start_, base + start_ + width)
            v_cols = slice(W + base + start_, W + base + start_ + width)
            g_win = go[:, 128 + base + start_ : 128 + base + start_ + width]
            v_head = kv[own, v_cols] * window_mask(i).astype(BF16)
            delta = go[:, head : head + 1].astype(F32) + go[:, H + head : H + head + 1].astype(F32)
            slopes = dot(g_win, v_head, 1, 1)
            weights = probs_k[head]
            dscore = (weights.astype(F32) * ((slopes - delta) * SCALE)).astype(BF16)
            d_k.append(dot(dscore, q_all[:, cols], 0, 0))
            d_v.append(dot(weights, g_win, 0, 0))
        out_v[:, W + base : W + base + GROUP] = join_heads(d_k).astype(BF16)
        out_v[:, 2 * W + base : 2 * W + base + GROUP] = join_heads(d_v).astype(BF16)

    query_group(0)
    wait(two_hop)
    s_up[0:half] = (keep_up[...] + r_2hop[0:half].astype(F32)).astype(BF16)
    one_hop += start([far(s_up.at[0:half], r_up.at[0:half], 5, up)])
    s_down[half:T] = (keep_down[...] + r_2hop[half:T].astype(F32)).astype(BF16)
    one_hop += start([far(s_down.at[half:T], r_down.at[half:T], 6, down)])

    query_group(1)
    wait(q_copies)
    probs_group(0)
    probs_group(1)

    wait(one_hop)
    grad_copies.append(send_grads(last, 20))
    second_copies = []
    for s in range(4):
        rows = pl.ds(pl.multiple_of((second + 1 + s) % 4 * 48, 16), 48)
        total = own_1[rows, :] + r_up[rows, :].astype(F32) + r_down[rows, :].astype(F32)
        if s < 3:
            s_2[s] = total.astype(BF16)
            second_copies += start([far(s_2.at[s], r_2.at[s], 7 + s, second_peers[s])])
        else:
            own_2[...] = total

    wait(grad_copies[0])
    key_group(0)

    wait(second_copies)
    total = own_2[...]
    for e in range(3):
        total = total + r_2[e].astype(F32)
    for part in range(8):
        s_3[part, 0:6, :] = total[part * 6 : part * 6 + 6]
    z_copies = []
    for e, (peer, part) in enumerate(z_peers):
        z_copies += start([far(s_3.at[part], r_3.at[e], 19 + e, peer)])

    wait(grad_copies[1])
    key_group(1)
    out_qkv = start([local(out_v, dqkv_h.at[0], 7)])

    wait(z_copies)
    total = s_3[zl * 4 + zh]
    for e in range(7):
        total = total + r_3[e]
    sums_o[...] = total
    wait(out_resid)
    wait(out_qkv)


def hand_over(dres_i, dqkv_i, sums_i, dres_o, dqkv_o, dproj_o, dker_o, sem):
    copies = [
        pltpu.make_async_copy(dres_i, dres_o, sem.at[0]),
        pltpu.make_async_copy(dqkv_i, dqkv_o, sem.at[1]),
    ]
    for copy in copies:
        copy.start()
    dproj_o[...] = sums_i[0:6, 0:W]
    dker_o[...] = sums_i[0:6, W : W + TAPS]
    for copy in copies:
        copy.wait()


def local(resid, qkv, cotangent, lengths, out_proj, ker):
    hbm = pl.BlockSpec(memory_space=pl.ANY)
    vmem = pl.BlockSpec(memory_space=pltpu.VMEM)
    scratch = [
        ((KEYS, W), BF16), ((KEYS, 2 * W), BF16), ((T, D), BF16), ((T, D), BF16),
        ((W, D), BF16), ((TAPS, D), F32), ((H, T, KEYS), BF16), ((H, KEYS, T), BF16),
        ((KEYS, 128), F32), ((256, W), BF16), ((256, W), BF16), ((KEYS, RW), BF16),
        ((CHUNKS, T + 2 * REACH, 128), F32), ((CHUNKS, T + 2 * EDGE, 128), F32), ((T, D), BF16),
        ((T, 3 * W), BF16),
        ((2, REACH, D), BF16), ((2, REACH, D), BF16), ((2, EDGE, D), BF16),
        ((128, 128), F32), ((CHUNKS, 8 * TAPS, 128), F32), ((D, 128), F32), ((D, 256), F32),
        ((16, 48, 256), BF16), ((16, 48, 384), BF16), ((16, 48, 384), BF16),
        ((T, RW), BF16), ((T, RW), BF16), ((T, RW), BF16), ((T, RW), BF16),
        ((T // 2, RW), F32), ((T // 2, RW), F32), ((T, RW), BF16), ((T, RW), BF16),
        ((T, RW), F32),
        ((3, 48, RW), BF16), ((3, 48, RW), BF16), ((48, RW), F32),
        ((8, 8, RW), F32), ((7, 8, RW), F32),
    ]
    dres, dqkv, sums = pl.pallas_call(
        kernel,
        out_shape=[
            jax.ShapeDtypeStruct((1, T, D), BF16),
            jax.ShapeDtypeStruct((1, T, 3 * W), BF16),
            jax.ShapeDtypeStruct((8, RW), F32),
        ],
        in_specs=[hbm, hbm, hbm, pl.BlockSpec(memory_space=pltpu.SMEM), hbm, hbm],
        out_specs=[hbm, hbm, vmem],
        scratch_shapes=[pltpu.VMEM(shape, kind) for shape, kind in scratch]
        + [
            pltpu.SemaphoreType.DMA((8,)),
            pltpu.SemaphoreType.DMA((22,)),
            pltpu.SemaphoreType.DMA((22,)),
            pltpu.SemaphoreType.DMA((26,)),
            pltpu.SemaphoreType.DMA((26,)),
        ],
        compiler_params=pltpu.CompilerParams(
            collective_id=0, has_side_effects=True, vmem_limit_bytes=56 * 2**20
        ),
        cost_estimate=pl.CostEstimate(
            flops=3_000_000_000, bytes_accessed=8_000_000, transcendentals=1_000_000
        ),
    )(resid, qkv, cotangent, lengths, out_proj, ker)
    dres, dqkv, dproj, dker = pl.pallas_call(
        hand_over,
        out_shape=[
            jax.ShapeDtypeStruct((1, T, D), BF16),
            jax.ShapeDtypeStruct((1, T, 3 * W), BF16),
            jax.ShapeDtypeStruct((6, W), F32),
            jax.ShapeDtypeStruct((6, TAPS), F32),
        ],
        in_specs=[vmem, vmem, vmem],
        out_specs=[hbm, hbm, vmem, vmem],
        scratch_shapes=[pltpu.SemaphoreType.DMA((2,))],
        cost_estimate=pl.CostEstimate(flops=0, bytes_accessed=4_000_000, transcendentals=0),
    )(dres, dqkv, sums)
    return dres, dqkv, dproj.T, dker.T


def solution(mesh):
    in_specs = (P("dp", "tm", None), P("dp", "tm", None), P("dp", "tm", None), P("dp"), P(), P())
    out_specs = (
        P("dp", "tm", None),
        P("dp", "tm", None),
        P(None, ("tm", "dp")),
        P(None, ("tm", "dp")),
    )
    return jax.shard_map(local, mesh=mesh, in_specs=in_specs, out_specs=out_specs, check_vma=False)
```

```python
import jax
import jax.numpy as jnp
from jax import lax
from jax.experimental import pallas as pl
from jax.experimental.pallas import tpu as pltpu
from jax.sharding import PartitionSpec as P

H = 8
HD = 96
T = 192
D = 1536
W = 768
TAPS = 31
CHUNKS = D // 128
EDGE = 16
REACH = 2 * EDGE
RW = W + 128
KEYS = 3 * T
GROUP = 4 * HD
WINDOWS = ((0, 128), (0, 256), (128, 256), (256, 128))
NEG_FILL = -1000000000.0
SCALE = HD ** (-0.5)
LOG2E = 1.4426950408889634
MESH = pl.DeviceIdType.MESH
F32 = jnp.float32
BF16 = jnp.bfloat16


def dot(a, b, ca, cb):
    return lax.dot_general(a, b, (((ca,), (cb,)), ((), ())), preferred_element_type=F32)


def window_mask(i):
    start, width = WINDOWS[i]
    lane = lax.broadcasted_iota(jnp.int32, (1, width), 1) + start
    return ((lane >= i * HD) & (lane < (i + 1) * HD)).astype(F32)


def join_heads(parts):
    lane = lax.broadcasted_iota(jnp.int32, (1, 128), 1)
    first = jnp.where(lane < 96, parts[0], parts[1][:, :128])
    second = jnp.where(lane < 64, parts[1][:, 128:], parts[2][:, :128])
    third = jnp.where(lane < 32, parts[2][:, 128:], parts[3])
    return jnp.concatenate([first, second, third], axis=1)


def lanes(c, width):
    return pl.ds(pl.multiple_of(c * width, width), width)


def kernel(
    resid_h, qkv_h, cot_h, len_s, proj_h, ker_h,
    dres_v, out_v, sums_o,
    q_all, kv, res_v, cot_v, w_v, ker_v, probs, probs_k, stat, att_v, att_m, go,
    mext, gext, hs, hm, hc, kt_part, lhs_own, lhs_out, lhs_in,
    s_2hop, r_2hop, s_up, s_down, keep_up, keep_down, r_up, r_down, own_1,
    s_2, r_2, own_2, s_3, r_3,
    loc_sem, nb_send, nb_recv, rs_send, rs_recv,
):
    tm = lax.axis_index("tm")
    zh = lax.axis_index("dp")
    core = tm % 2
    zl = (tm // 2) % 2
    x = (tm // 4) % 4
    y = tm // 16
    other = 1 - core
    zz = zh * 2 + zl

    def device(y_, x_, zl_, core_, zh_):
        return {"tm": ((y_ * 4 + x_) * 2 + zl_) * 2 + core_, "dp": zh_}

    left = {"tm": (tm + 63) % 64, "dp": zh}
    right = {"tm": (tm + 1) % 64, "dp": zh}
    mate = device(y, x, zl, other, zh)
    up = device((y + other) % 4, (x + core) % 4, zl, core, zh)
    down = device((y + 3 * other) % 4, (x + 3 * core) % 4, zl, core, zh)
    second_peers = [device((y + e * core) % 4, (x + e * other) % 4, zl, core, zh) for e in (1, 2, 3)]
    z_peers = []
    for e in range(1, 8):
        z_to = (zz + e) % 8
        z_peers.append((device(y, x, z_to % 2, core, z_to // 2), (z_to % 2) * 4 + z_to // 2))

    def local(src, dst, i):
        return pltpu.make_async_copy(src, dst, loc_sem.at[i])

    def near(src, dst, i, to):
        return pltpu.make_async_remote_copy(
            src_ref=src, dst_ref=dst, send_sem=nb_send.at[i], recv_sem=nb_recv.at[i],
            device_id=to, device_id_type=MESH,
        )

    def far(src, dst, i, to):
        return pltpu.make_async_remote_copy(
            src_ref=src, dst_ref=dst, send_sem=rs_send.at[i], recv_sem=rs_recv.at[i],
            device_id=to, device_id_type=MESH,
        )

    def start(copies):
        for copy in copies:
            copy.start()
        return copies

    def wait(copies):
        for copy in copies:
            copy.wait()

    low, own, high = slice(0, T), slice(T, 2 * T), slice(2 * T, 3 * T)

    ins = start([
        local(qkv_h.at[0, :, 0:W], q_all.at[own], 0),
        local(qkv_h.at[0, :, W : 3 * W], kv.at[own], 1),
        local(proj_h, w_v, 2),
        local(resid_h.at[0], res_v, 3),
        local(cot_h.at[0], cot_v, 4),
        local(ker_h, ker_v, 5),
    ])

    barrier = pltpu.get_barrier_semaphore()
    everyone = [left, right, up, down] + second_peers + [peer for peer, _ in z_peers]
    for peer in everyone:
        pl.semaphore_signal(barrier, inc=1, device_id=peer, device_id_type=MESH)
    pl.semaphore_wait(barrier, len(everyone))

    kv_copies = []
    for group in range(2):
        for part in range(2):
            cols = slice(part * W + group * GROUP, part * W + (group + 1) * GROUP)
            src = qkv_h.at[0, :, W + cols.start : W + cols.stop]
            i = group * 4 + part * 2
            kv_copies.append(near(src, kv.at[low, cols], i, right))
            kv_copies.append(near(src, kv.at[high, cols], i + 1, left))
    start(kv_copies)

    length = len_s[0]
    first_frame = tm * T
    frame = first_frame + lax.broadcasted_iota(jnp.int32, (T, 1), 0)
    valid = (frame < length).astype(F32)
    key = first_frame - T + lax.broadcasted_iota(jnp.int32, (1, KEYS), 1)
    key_open = (key >= 0) & (key < length)
    own_key = first_frame + lax.broadcasted_iota(jnp.int32, (1, T), 1)
    near_query = first_frame - T + lax.broadcasted_iota(jnp.int32, (KEYS, 1), 0)
    pair_open = (own_key < length) & (near_query >= 0) & (near_query < 64 * T)
    has_left = (tm > 0).astype(F32)
    has_right = (tm < 63).astype(F32)
    lane = lax.broadcasted_iota(jnp.int32, (1, 128), 1)

    eye_row = lax.broadcasted_iota(jnp.int32, (256 - T, 128), 0)
    eye_col = lax.broadcasted_iota(jnp.int32, (256 - T, 128), 1)
    att_v[T:256, 0:W] = jnp.zeros((256 - T, W), BF16)
    att_v[0:T, W:RW] = jnp.zeros((T, 128), BF16)
    att_v[T:256, W:RW] = ((eye_row == eye_col) & (eye_row < 32)).astype(F32).astype(BF16)
    dres_v[T:256, :] = jnp.zeros((256 - T, D), BF16)
    s_3[...] = jnp.zeros_like(s_3)

    wait(ins)
    wait(kv_copies[:4])

    def forward_group(group, stats):
        base = group * GROUP
        outs = []
        for i in range(4):
            start_, width = WINDOWS[i]
            cols = slice(base + start_, base + start_ + width)
            v_cols = slice(W + base + start_, W + base + start_ + width)
            q_head = q_all[own, cols] * window_mask(i).astype(BF16)
            scores = dot(q_head, kv[:, cols], 1, 1)
            scores = jnp.where(key_open, scores * (SCALE * LOG2E), NEG_FILL)
            peak = jnp.max(scores, axis=1, keepdims=True)
            weights = jnp.exp2(scores - peak)
            total = jnp.sum(weights, axis=1, keepdims=True)
            weights = (weights * (1.0 / total)).astype(BF16)
            probs[group * 4 + i] = weights
            stats = jnp.where(lane == group * 4 + i, peak + jnp.log2(total), stats)
            outs.append(dot(weights, kv[:, v_cols], 1, 0))
        att_v[0:T, base : base + GROUP] = (join_heads(outs) * valid).astype(BF16)
        return stats

    stats = forward_group(0, jnp.zeros((T, 128), F32))
    wait(kv_copies[4:])
    early = start([
        near(cot_v.at[0:EDGE], hc.at[1], 8, left),
        near(cot_v.at[T - EDGE : T], hc.at[0], 9, right),
    ])
    q_copies = start([
        near(q_all.at[own, 0:GROUP], q_all.at[low, 0:GROUP], 10, right),
        near(q_all.at[own, 0:GROUP], q_all.at[high, 0:GROUP], 11, left),
    ])
    stat[own, :] = forward_group(1, stats)
    early += start([far(att_v, att_m, 0, mate)])

    def project(j, carry):
        cols = lanes(j, 256)
        mixed = res_v[:, cols].astype(F32) + dot(att_v[0:T, 0:W], w_v[:, cols], 1, 0)
        masked = (mixed.astype(BF16).astype(F32) * valid).astype(BF16)
        hs[0, :, cols] = masked[0:REACH]
        hs[1, :, cols] = masked[T - REACH : T]
        wide = masked.astype(F32)
        mext[2 * j, REACH : REACH + T, :] = wide[:, :128]
        mext[2 * j + 1, REACH : REACH + T, :] = wide[:, 128:]
        return carry

    lax.fori_loop(0, D // 256, project, 0)
    mask_halo = start([near(hs.at[0], hm.at[1], 12, left), near(hs.at[1], hm.at[0], 13, right)])

    def windows(src, c, first, count):
        for s in range(8):
            taps = range(s, TAPS, 8)
            window = src[c, first + s : first + s + count + 8 * (len(taps) - 1), :]
            for place, j in enumerate(taps):
                yield j, window[8 * place : 8 * place + count]

    def convolve(src, c, first, count, flip):
        total = None
        for j, rows in windows(src, c, first, count):
            tap = TAPS - 1 - j if flip else j
            term = ker_v[tap : tap + 1, lanes(c, 128)] * rows
            total = term if total is None else total + term
        return total

    def conv_rows(c, row, count, cot):
        conv = convolve(mext, c, row + REACH - 15, count, False)
        sigma = jax.nn.sigmoid(conv)
        slope = sigma * (1.0 + conv * (1.0 - sigma))
        grad = (cot * slope).astype(BF16).astype(F32)
        gext[c, EDGE + row : EDGE + row + count, :] = grad

    def back_rows(c, row, count):
        cols = lanes(c, 128)
        back = convolve(gext, c, row + EDGE - 15, count, True)
        cot = cot_v[row : row + count, cols].astype(F32)
        dres_v[row : row + count, cols] = (cot + valid[row : row + count] * back).astype(BF16)

    def kernel_terms(c, row, count, sums):
        grad = gext[c, EDGE + row : EDGE + row + count, :]
        for j, rows in windows(mext, c, row + REACH - 15, count):
            term = jnp.sum((grad * rows).reshape(count // 8, 8, 128), axis=0)
            sums[j] = term if sums[j] is None else sums[j] + term

    def conv_inner(c, carry):
        for row in (16, 96):
            conv_rows(c, row, 80, cot_v[row : row + 80, lanes(c, 128)].astype(F32))
        sums = [None] * TAPS
        for row in (16, 96):
            kernel_terms(c, row, 80, sums)
        for j in range(TAPS):
            kt_part[c, 8 * j : 8 * j + 8, :] = sums[j]
        back_rows(c, 32, 64)
        back_rows(c, 96, 64)
        return carry

    lax.fori_loop(0, CHUNKS // 2, conv_inner, 0)
    q_copies += start([
        near(q_all.at[own, GROUP:W], q_all.at[low, GROUP:W], 14, right),
        near(q_all.at[own, GROUP:W], q_all.at[high, GROUP:W], 15, left),
        near(stat.at[own], stat.at[low], 16, right),
        near(stat.at[own], stat.at[high], 17, left),
    ])
    lax.fori_loop(CHUNKS // 2, CHUNKS, conv_inner, 0)
    wait(early)
    wait(mask_halo)

    def edges_and_back(c):
        cols = lanes(c, 128)
        mext[c, 0:REACH, :] = hm[0, :, cols].astype(F32) * has_left
        mext[c, REACH + T : 2 * REACH + T, :] = hm[1, :, cols].astype(F32) * has_right
        cot = cot_v[0:EDGE, cols].astype(F32)
        before = hc[0, :, cols].astype(F32) * has_left
        conv_rows(c, -EDGE, REACH, jnp.concatenate([before, cot], axis=0))
        cot = cot_v[T - EDGE : T, cols].astype(F32)
        after = hc[1, :, cols].astype(F32) * has_right
        conv_rows(c, T - EDGE, REACH, jnp.concatenate([cot, after], axis=0))
        sums = [kt_part[c, 8 * j : 8 * j + 8, :] for j in range(TAPS)]
        kernel_terms(c, 0, EDGE, sums)
        kernel_terms(c, T - EDGE, EDGE, sums)
        for j in range(TAPS):
            kt_part[c, 8 * j : 8 * j + 8, :] = sums[j]
        back_rows(c, 0, 32)
        back_rows(c, T - 32, 32)

    tap_row = lax.broadcasted_iota(jnp.int32, (32, 8 * TAPS), 0)
    tap_col = lax.broadcasted_iota(jnp.int32, (32, 8 * TAPS), 1)
    adder = (tap_col // 8 == tap_row).astype(F32).astype(BF16)

    def pair_copy(q):
        quarter = pl.ds(4 * q, 4)
        return far(lhs_out.at[quarter], lhs_in.at[quarter], 15 + q, mate)

    def finish(q):
        cols = lanes(q, 384)
        terms = jnp.concatenate([kt_part[3 * q + i].astype(BF16) for i in range(3)], axis=1)
        dres_v[T : T + 32, cols] = dot(adder, terms, 1, 0).astype(BF16)
        turned = dres_v[:, cols].T.astype(F32)
        for part in range(4):
            row = 96 * part
            both = [
                jnp.concatenate(
                    [turned[row + 24 * i : row + 24 * i + 24], turned[row + 48 + 24 * i : row + 72 + 24 * i]],
                    axis=0,
                )
                for i in range(2)
            ]
            lhs_own[4 * q + part] = jnp.where(core == 0, both[0], both[1]).astype(BF16)
            lhs_out[4 * q + part] = jnp.where(core == 0, both[1], both[0]).astype(BF16)
        pair_copy(q).start()

    def one_chunk(c, carry):
        edges_and_back(c)
        return carry

    def quarter(q, carry):
        lax.fori_loop(3 * q, 3 * q + 3, one_chunk, 0)
        finish(q)
        return carry

    lax.fori_loop(0, 4, quarter, 0)
    pair_copies = [pair_copy(q) for q in range(4)]

    place, second = y * other + x * core, x * other + y * core

    def attended_grad(j, carry):
        go[own, pl.ds(pl.multiple_of(128 + j * 256, 128), 256)] = (
            valid * dot(dres_v[0:T, :], w_v[lanes(j, 256), :], 1, 1)
        ).astype(BF16)
        return carry

    lax.fori_loop(0, W // 256, attended_grad, 0)
    deltas = jnp.zeros((T, 128), F32)
    for head in range(H):
        start_, width = WINDOWS[head % 4]
        first = head // 4 * GROUP + start_
        product = (
            go[own, 128 + first : 128 + first + width].astype(F32)
            * att_v[0:T, first : first + width].astype(F32)
        )
        delta = jnp.sum(product * window_mask(head % 4), axis=1, keepdims=True)
        coarse = delta.astype(BF16).astype(F32)
        deltas = jnp.where(lane == head, coarse, deltas)
        deltas = jnp.where(lane == H + head, delta - coarse, deltas)
    go[own, 0:128] = deltas.astype(BF16)
    first, last = slice(0, 128 + GROUP), slice(128 + GROUP, 128 + W)

    def send_grads(cols, i):
        return start([
            near(go.at[own, cols], go.at[low, cols], i, right),
            near(go.at[own, cols], go.at[high, cols], i + 1, left),
        ])

    grad_copies = [send_grads(first, 18)]

    wait(pair_copies)

    def pair_sum(a):
        blocks = [(a * other + b * core) * 4 + b * other + a * core for b in range(4)]
        mine = jnp.concatenate([lhs_own[block] for block in blocks], axis=0)
        theirs = jnp.concatenate([lhs_in[block] for block in blocks], axis=0)
        return dot(mine, att_v[...], 1, 0) + dot(theirs, att_m[...], 1, 0)

    half = 96
    whole = pair_sum((place + 2) % 4)
    s_2hop[0:half] = whole[0:half].astype(BF16)
    s_2hop[half:T] = whole[half:T].astype(BF16)
    two_hop = start([
        far(s_2hop.at[0:half], r_2hop.at[0:half], 1, up),
        far(s_2hop.at[half:T], r_2hop.at[half:T], 2, down),
    ])
    whole = pair_sum((place + 1) % 4)
    keep_up[...] = whole[0:half]
    s_up[half:T] = whole[half:T].astype(BF16)
    one_hop = start([far(s_up.at[half:T], r_up.at[half:T], 3, up)])
    whole = pair_sum((place + 3) % 4)
    s_down[0:half] = whole[0:half].astype(BF16)
    keep_down[...] = whole[half:T]
    one_hop += start([far(s_down.at[0:half], r_down.at[0:half], 4, down)])
    own_1[...] = pair_sum(place)

    def query_group(group):
        base = group * GROUP
        d_q = []
        for i in range(4):
            head = group * 4 + i
            start_, width = WINDOWS[i]
            cols = slice(base + start_, base + start_ + width)
            v_cols = slice(W + base + start_, W + base + start_ + width)
            g_cols = slice(128 + base + start_, 128 + base + start_ + width)
            g_head = go[own, g_cols] * window_mask(i).astype(BF16)
            delta = go[own, head : head + 1].astype(F32) + go[own, H + head : H + head + 1].astype(F32)
            slopes = dot(g_head, kv[:, v_cols], 1, 1)
            dscore = (probs[head].astype(F32) * ((slopes - delta) * SCALE)).astype(BF16)
            d_q.append(dot(dscore, kv[:, cols], 1, 0))
        out_v[:, base : base + GROUP] = join_heads(d_q).astype(BF16)

    def probs_group(group):
        base = group * GROUP
        for i in range(4):
            head = group * 4 + i
            start_, width = WINDOWS[i]
            cols = slice(base + start_, base + start_ + width)
            k_head = kv[own, cols] * window_mask(i).astype(BF16)
            scores = dot(q_all[:, cols], k_head, 1, 1)
            scores = jnp.where(pair_open, scores * (SCALE * LOG2E), NEG_FILL)
            probs_k[head] = jnp.exp2(scores - stat[:, head : head + 1]).astype(BF16)

    def key_group(group):
        base = group * GROUP
        d_k, d_v = [], []
        for i in range(4):
            head = group * 4 + i
            start_, width = WINDOWS[i]
            cols = slice(base + start_, base + start_ + width)
            v_cols = slice(W + base + start_, W + base + start_ + width)
            g_win = go[:, 128 + base + start_ : 128 + base + start_ + width]
            v_head = kv[own, v_cols] * window_mask(i).astype(BF16)
            delta = go[:, head : head + 1].astype(F32) + go[:, H + head : H + head + 1].astype(F32)
            slopes = dot(g_win, v_head, 1, 1)
            weights = probs_k[head]
            dscore = (weights.astype(F32) * ((slopes - delta) * SCALE)).astype(BF16)
            d_k.append(dot(dscore, q_all[:, cols], 0, 0))
            d_v.append(dot(weights, g_win, 0, 0))
        out_v[:, W + base : W + base + GROUP] = join_heads(d_k).astype(BF16)
        out_v[:, 2 * W + base : 2 * W + base + GROUP] = join_heads(d_v).astype(BF16)

    query_group(0)
    wait(two_hop)
    s_up[0:half] = (keep_up[...] + r_2hop[0:half].astype(F32)).astype(BF16)
    one_hop += start([far(s_up.at[0:half], r_up.at[0:half], 5, up)])
    s_down[half:T] = (keep_down[...] + r_2hop[half:T].astype(F32)).astype(BF16)
    one_hop += start([far(s_down.at[half:T], r_down.at[half:T], 6, down)])

    query_group(1)
    wait(q_copies)
    probs_group(0)
    probs_group(1)

    wait(one_hop)
    grad_copies.append(send_grads(last, 20))
    second_copies = []
    for s in range(4):
        rows = pl.ds(pl.multiple_of((second + 1 + s) % 4 * 48, 16), 48)
        total = own_1[rows, :] + r_up[rows, :].astype(F32) + r_down[rows, :].astype(F32)
        if s < 3:
            s_2[s] = total.astype(BF16)
            second_copies += start([far(s_2.at[s], r_2.at[s], 7 + s, second_peers[s])])
        else:
            own_2[...] = total

    wait(grad_copies[0])
    key_group(0)

    wait(second_copies)
    total = own_2[...]
    for e in range(3):
        total = total + r_2[e].astype(F32)
    for part in range(8):
        s_3[part, 0:6, :] = total[part * 6 : part * 6 + 6]
    z_copies = []
    for e, (peer, part) in enumerate(z_peers):
        z_copies += start([far(s_3.at[part], r_3.at[e], 19 + e, peer)])

    wait(grad_copies[1])
    key_group(1)

    wait(z_copies)
    total = s_3[zl * 4 + zh]
    for e in range(7):
        total = total + r_3[e]
    sums_o[...] = total


def hand_over(dres_i, dqkv_i, sums_i, dres_o, dqkv_o, dproj_o, dker_o, sem):
    copies = [
        pltpu.make_async_copy(dres_i.at[0:T], dres_o.at[0], sem.at[0]),
        pltpu.make_async_copy(dqkv_i, dqkv_o.at[0], sem.at[1]),
    ]
    for copy in copies:
        copy.start()
    dproj_o[...] = sums_i[0:6, 0:W]
    dker_o[...] = sums_i[0:6, W : W + TAPS]
    for copy in copies:
        copy.wait()


def local(resid, qkv, cotangent, lengths, out_proj, ker):
    hbm = pl.BlockSpec(memory_space=pl.ANY)
    vmem = pl.BlockSpec(memory_space=pltpu.VMEM)
    scratch = [
        ((KEYS, W), BF16), ((KEYS, 2 * W), BF16), ((T, D), BF16), ((T, D), BF16),
        ((W, D), BF16), ((TAPS, D), F32), ((H, T, KEYS), BF16), ((H, KEYS, T), BF16),
        ((KEYS, 128), F32), ((256, RW), BF16), ((256, RW), BF16), ((KEYS, RW), BF16),
        ((CHUNKS, T + 2 * REACH, 128), F32), ((CHUNKS, T + 2 * EDGE, 128), F32),
        ((2, REACH, D), BF16), ((2, REACH, D), BF16), ((2, EDGE, D), BF16),
        ((CHUNKS, 8 * TAPS, 128), F32),
        ((16, 48, 256), BF16), ((16, 48, 256), BF16), ((16, 48, 256), BF16),
        ((T, RW), BF16), ((T, RW), BF16), ((T, RW), BF16), ((T, RW), BF16),
        ((T // 2, RW), F32), ((T // 2, RW), F32), ((T, RW), BF16), ((T, RW), BF16),
        ((T, RW), F32),
        ((3, 48, RW), BF16), ((3, 48, RW), BF16), ((48, RW), F32),
        ((8, 8, RW), F32), ((7, 8, RW), F32),
    ]
    dres, dqkv, sums = pl.pallas_call(
        kernel,
        out_shape=[
            pltpu.VMEM((256, D), BF16),
            pltpu.VMEM((T, 3 * W), BF16),
            pltpu.VMEM((8, RW), F32),
        ],
        in_specs=[hbm, hbm, hbm, pl.BlockSpec(memory_space=pltpu.SMEM), hbm, hbm],
        out_specs=[vmem, vmem, vmem],
        scratch_shapes=[pltpu.VMEM(shape, kind) for shape, kind in scratch]
        + [
            pltpu.SemaphoreType.DMA((8,)),
            pltpu.SemaphoreType.DMA((22,)),
            pltpu.SemaphoreType.DMA((22,)),
            pltpu.SemaphoreType.DMA((26,)),
            pltpu.SemaphoreType.DMA((26,)),
        ],
        compiler_params=pltpu.CompilerParams(
            collective_id=0, has_side_effects=True, vmem_limit_bytes=60 * 2**20
        ),
        cost_estimate=pl.CostEstimate(
            flops=3_000_000_000, bytes_accessed=8_000_000, transcendentals=1_000_000
        ),
    )(resid, qkv, cotangent, lengths, out_proj, ker)
    dres, dqkv, dproj, dker = pl.pallas_call(
        hand_over,
        out_shape=[
            jax.ShapeDtypeStruct((1, T, D), BF16),
            jax.ShapeDtypeStruct((1, T, 3 * W), BF16),
            jax.ShapeDtypeStruct((6, W), F32),
            jax.ShapeDtypeStruct((6, TAPS), F32),
        ],
        in_specs=[vmem, vmem, vmem],
        out_specs=[hbm, hbm, vmem, vmem],
        scratch_shapes=[pltpu.SemaphoreType.DMA((2,))],
        compiler_params=pltpu.CompilerParams(vmem_limit_bytes=8 * 2**20),
        cost_estimate=pl.CostEstimate(flops=0, bytes_accessed=4_000_000, transcendentals=0),
    )(dres, dqkv, sums)
    return dres, dqkv, dproj.T, dker.T


def solution(mesh):
    in_specs = (P("dp", "tm", None), P("dp", "tm", None), P("dp", "tm", None), P("dp"), P(), P())
    out_specs = (
        P("dp", "tm", None),
        P("dp", "tm", None),
        P(None, ("tm", "dp")),
        P(None, ("tm", "dp")),
    )
    return jax.shard_map(local, mesh=mesh, in_specs=in_specs, out_specs=out_specs, check_vma=False)
```

```python
import jax
import jax.numpy as jnp
from jax import lax
from jax.experimental import pallas as pl
from jax.experimental.pallas import tpu as pltpu
from jax.sharding import PartitionSpec as P

H = 8
HD = 96
T = 192
D = 1536
W = 768
TAPS = 31
CHUNKS = D // 128
EDGE = 16
REACH = 2 * EDGE
RW = W + 128
KEYS = 3 * T
GROUP = 4 * HD
WINDOWS = ((0, 128), (0, 256), (128, 256), (256, 128))
NEG_FILL = -1000000000.0
SCALE = HD ** (-0.5)
LOG2E = 1.4426950408889634
MESH = pl.DeviceIdType.MESH
F32 = jnp.float32
BF16 = jnp.bfloat16


def dot(a, b, ca, cb):
    return lax.dot_general(a, b, (((ca,), (cb,)), ((), ())), preferred_element_type=F32)


def window_mask(i):
    start, width = WINDOWS[i]
    lane = lax.broadcasted_iota(jnp.int32, (1, width), 1) + start
    return ((lane >= i * HD) & (lane < (i + 1) * HD)).astype(F32)


def join_heads(parts):
    lane = lax.broadcasted_iota(jnp.int32, (1, 128), 1)
    first = jnp.where(lane < 96, parts[0], parts[1][:, :128])
    second = jnp.where(lane < 64, parts[1][:, 128:], parts[2][:, :128])
    third = jnp.where(lane < 32, parts[2][:, 128:], parts[3])
    return jnp.concatenate([first, second, third], axis=1)


def lanes(c, width):
    return pl.ds(pl.multiple_of(c * width, width), width)


def kernel(
    resid_h, qkv_h, cot_h, len_s, proj_h, ker_h,
    dres_v, out_v, sums_o,
    q_all, kv, res_v, cot_v, w_v, ker_v, probs, probs_k, stat, att_v, att_m, go,
    mext, gext, hs, hm, hc, mix, kt_part, lhs_own, lhs_out, lhs_in,
    s_2hop, r_2hop, s_up, s_down, keep_up, keep_down, r_up, r_down, own_1,
    s_2, r_2, own_2, s_3, r_3,
    loc_sem, nb_send, nb_recv, rs_send, rs_recv,
):
    tm = lax.axis_index("tm")
    zh = lax.axis_index("dp")
    core = tm % 2
    zl = (tm // 2) % 2
    x = (tm // 4) % 4
    y = tm // 16
    other = 1 - core
    zz = zh * 2 + zl

    def device(y_, x_, zl_, core_, zh_):
        return {"tm": ((y_ * 4 + x_) * 2 + zl_) * 2 + core_, "dp": zh_}

    left = {"tm": (tm + 63) % 64, "dp": zh}
    right = {"tm": (tm + 1) % 64, "dp": zh}
    mate = device(y, x, zl, other, zh)
    up = device((y + other) % 4, (x + core) % 4, zl, core, zh)
    down = device((y + 3 * other) % 4, (x + 3 * core) % 4, zl, core, zh)
    second_peers = [device((y + e * core) % 4, (x + e * other) % 4, zl, core, zh) for e in (1, 2, 3)]
    z_peers = []
    for e in range(1, 8):
        z_to = (zz + e) % 8
        z_peers.append((device(y, x, z_to % 2, core, z_to // 2), (z_to % 2) * 4 + z_to // 2))

    def local(src, dst, i):
        return pltpu.make_async_copy(src, dst, loc_sem.at[i])

    def near(src, dst, i, to):
        return pltpu.make_async_remote_copy(
            src_ref=src, dst_ref=dst, send_sem=nb_send.at[i], recv_sem=nb_recv.at[i],
            device_id=to, device_id_type=MESH,
        )

    def far(src, dst, i, to):
        return pltpu.make_async_remote_copy(
            src_ref=src, dst_ref=dst, send_sem=rs_send.at[i], recv_sem=rs_recv.at[i],
            device_id=to, device_id_type=MESH,
        )

    def start(copies):
        for copy in copies:
            copy.start()
        return copies

    def wait(copies):
        for copy in copies:
            copy.wait()

    low, own, high = slice(0, T), slice(T, 2 * T), slice(2 * T, 3 * T)

    ins = start([
        local(qkv_h.at[0, :, 0:W], q_all.at[own], 0),
        local(qkv_h.at[0, :, W : 3 * W], kv.at[own], 1),
        local(proj_h, w_v, 2),
        local(resid_h.at[0], res_v, 3),
        local(cot_h.at[0], cot_v, 4),
        local(ker_h, ker_v, 5),
    ])

    barrier = pltpu.get_barrier_semaphore()
    everyone = [left, right, up, down] + second_peers + [peer for peer, _ in z_peers]
    for peer in everyone:
        pl.semaphore_signal(barrier, inc=1, device_id=peer, device_id_type=MESH)

    pl.semaphore_wait(barrier, len(everyone))

    kv_copies = []
    for group in range(2):
        for part in range(2):
            cols = slice(part * W + group * GROUP, part * W + (group + 1) * GROUP)
            src = qkv_h.at[0, :, W + cols.start : W + cols.stop]
            i = group * 4 + part * 2
            kv_copies.append(near(src, kv.at[low, cols], i, right))
            kv_copies.append(near(src, kv.at[high, cols], i + 1, left))
    start(kv_copies)

    length = len_s[0]
    first_frame = tm * T
    frame = first_frame + lax.broadcasted_iota(jnp.int32, (T, 1), 0)
    valid = (frame < length).astype(F32)
    key = first_frame - T + lax.broadcasted_iota(jnp.int32, (1, KEYS), 1)
    key_open = (key >= 0) & (key < length)
    own_key = first_frame + lax.broadcasted_iota(jnp.int32, (1, T), 1)
    near_query = first_frame - T + lax.broadcasted_iota(jnp.int32, (KEYS, 1), 0)
    pair_open = (own_key < length) & (near_query >= 0) & (near_query < 64 * T)
    has_left = (tm > 0).astype(F32)
    has_right = (tm < 63).astype(F32)
    lane = lax.broadcasted_iota(jnp.int32, (1, 128), 1)

    eye_row = lax.broadcasted_iota(jnp.int32, (256 - T, 128), 0)
    eye_col = lax.broadcasted_iota(jnp.int32, (256 - T, 128), 1)
    att_v[T:256, 0:W] = jnp.zeros((256 - T, W), BF16)
    att_v[0:T, W:RW] = jnp.zeros((T, 128), BF16)
    att_v[T:256, W:RW] = ((eye_row == eye_col) & (eye_row < 32)).astype(F32).astype(BF16)
    dres_v[T:256, :] = jnp.zeros((256 - T, D), BF16)
    s_3[...] = jnp.zeros_like(s_3)

    wait(ins)
    wait(kv_copies[:4])

    def forward_group(group, stats):
        base = group * GROUP
        outs = []
        for i in range(4):
            start_, width = WINDOWS[i]
            cols = slice(base + start_, base + start_ + width)
            v_cols = slice(W + base + start_, W + base + start_ + width)
            q_head = q_all[own, cols] * window_mask(i).astype(BF16)
            scores = dot(q_head, kv[:, cols], 1, 1)
            scores = jnp.where(key_open, scores * (SCALE * LOG2E), NEG_FILL)
            peak = jnp.max(scores, axis=1, keepdims=True)
            weights = jnp.exp2(scores - peak)
            total = jnp.sum(weights, axis=1, keepdims=True)
            weights = (weights * (1.0 / total)).astype(BF16)
            probs[group * 4 + i] = weights
            stats = jnp.where(lane == group * 4 + i, peak + jnp.log2(total), stats)
            outs.append(dot(weights, kv[:, v_cols], 1, 0))
        att_v[0:T, base : base + GROUP] = (join_heads(outs) * valid).astype(BF16)
        return stats

    def project_half(j, carry):
        cols = lanes(j, 256)
        mix[:, cols] = res_v[:, cols].astype(F32) + dot(
            att_v[0:T, 0:GROUP], w_v[0:GROUP, cols], 1, 0
        )
        return carry

    stats = forward_group(0, jnp.zeros((T, 128), F32))
    lax.fori_loop(0, D // 256, project_half, 0)
    wait(kv_copies[4:])
    early = start([
        near(cot_v.at[0:EDGE], hc.at[1], 8, left),
        near(cot_v.at[T - EDGE : T], hc.at[0], 9, right),
    ])
    q_copies = start([
        near(q_all.at[own, 0:GROUP], q_all.at[low, 0:GROUP], 10, right),
        near(q_all.at[own, 0:GROUP], q_all.at[high, 0:GROUP], 11, left),
    ])
    stat[own, :] = forward_group(1, stats)
    early += start([far(att_v, att_m, 0, mate)])

    def project(j, carry):
        cols = lanes(j, 256)
        mixed = mix[:, cols] + dot(att_v[0:T, GROUP:W], w_v[GROUP:W, cols], 1, 0)
        masked = (mixed.astype(BF16).astype(F32) * valid).astype(BF16)
        hs[0, :, cols] = masked[0:REACH]
        hs[1, :, cols] = masked[T - REACH : T]
        wide = masked.astype(F32)
        mext[2 * j, REACH : REACH + T, :] = wide[:, :128]
        mext[2 * j + 1, REACH : REACH + T, :] = wide[:, 128:]
        return carry

    lax.fori_loop(0, D // 256, project, 0)
    mask_halo = start([near(hs.at[0], hm.at[1], 12, left), near(hs.at[1], hm.at[0], 13, right)])

    def windows(src, c, first, count):
        for s in range(8):
            taps = range(s, TAPS, 8)
            window = src[c, first + s : first + s + count + 8 * (len(taps) - 1), :]
            for place, j in enumerate(taps):
                yield j, window[8 * place : 8 * place + count]

    def convolve(src, c, first, count, flip):
        total = None
        for j, rows in windows(src, c, first, count):
            tap = TAPS - 1 - j if flip else j
            term = ker_v[tap : tap + 1, lanes(c, 128)] * rows
            total = term if total is None else total + term
        return total

    def conv_rows(c, row, count, cot):
        conv = convolve(mext, c, row + REACH - 15, count, False)
        sigma = jax.nn.sigmoid(conv)
        slope = sigma * (1.0 + conv * (1.0 - sigma))
        grad = (cot * slope).astype(BF16).astype(F32)
        gext[c, EDGE + row : EDGE + row + count, :] = grad

    def back_rows(c, row, count):
        cols = lanes(c, 128)
        back = convolve(gext, c, row + EDGE - 15, count, True)
        cot = cot_v[row : row + count, cols].astype(F32)
        dres_v[row : row + count, cols] = (cot + valid[row : row + count] * back).astype(BF16)

    def kernel_terms(c, row, count, sums):
        grad = gext[c, EDGE + row : EDGE + row + count, :]
        for j, rows in windows(mext, c, row + REACH - 15, count):
            term = jnp.sum((grad * rows).reshape(count // 8, 8, 128), axis=0)
            sums[j] = term if sums[j] is None else sums[j] + term

    def conv_inner(c, carry):
        for row in (16, 96):
            conv_rows(c, row, 80, cot_v[row : row + 80, lanes(c, 128)].astype(F32))
        sums = [None] * TAPS
        for row in (16, 96):
            kernel_terms(c, row, 80, sums)
        for j in range(TAPS):
            kt_part[c, 8 * j : 8 * j + 8, :] = sums[j]
        back_rows(c, 32, 64)
        back_rows(c, 96, 64)
        return carry

    lax.fori_loop(0, CHUNKS // 2, conv_inner, 0)
    q_copies += start([
        near(q_all.at[own, GROUP:W], q_all.at[low, GROUP:W], 14, right),
        near(q_all.at[own, GROUP:W], q_all.at[high, GROUP:W], 15, left),
        near(stat.at[own], stat.at[low], 16, right),
        near(stat.at[own], stat.at[high], 17, left),
    ])
    lax.fori_loop(CHUNKS // 2, CHUNKS, conv_inner, 0)
    wait(early)
    wait(mask_halo)

    def edges_and_back(c):
        cols = lanes(c, 128)
        mext[c, 0:REACH, :] = hm[0, :, cols].astype(F32) * has_left
        mext[c, REACH + T : 2 * REACH + T, :] = hm[1, :, cols].astype(F32) * has_right
        cot = cot_v[0:EDGE, cols].astype(F32)
        before = hc[0, :, cols].astype(F32) * has_left
        conv_rows(c, -EDGE, REACH, jnp.concatenate([before, cot], axis=0))
        cot = cot_v[T - EDGE : T, cols].astype(F32)
        after = hc[1, :, cols].astype(F32) * has_right
        conv_rows(c, T - EDGE, REACH, jnp.concatenate([cot, after], axis=0))
        sums = [kt_part[c, 8 * j : 8 * j + 8, :] for j in range(TAPS)]
        kernel_terms(c, 0, EDGE, sums)
        kernel_terms(c, T - EDGE, EDGE, sums)
        for j in range(TAPS):
            kt_part[c, 8 * j : 8 * j + 8, :] = sums[j]
        back_rows(c, 0, 32)
        back_rows(c, T - 32, 32)

    tap_row = lax.broadcasted_iota(jnp.int32, (32, 8 * TAPS), 0)
    tap_col = lax.broadcasted_iota(jnp.int32, (32, 8 * TAPS), 1)
    adder = (tap_col // 8 == tap_row).astype(F32).astype(BF16)

    def pair_copy(q):
        quarter = pl.ds(4 * q, 4)
        return far(lhs_out.at[quarter], lhs_in.at[quarter], 15 + q, mate)

    def finish(q):
        cols = lanes(q, 384)
        terms = jnp.concatenate([kt_part[3 * q + i].astype(BF16) for i in range(3)], axis=1)
        dres_v[T : T + 32, cols] = dot(adder, terms, 1, 0).astype(BF16)
        turned = dres_v[:, cols].T.astype(F32)
        for part in range(4):
            row = 96 * part
            both = [
                jnp.concatenate(
                    [turned[row + 24 * i : row + 24 * i + 24], turned[row + 48 + 24 * i : row + 72 + 24 * i]],
                    axis=0,
                )
                for i in range(2)
            ]
            lhs_own[4 * q + part] = jnp.where(core == 0, both[0], both[1]).astype(BF16)
            lhs_out[4 * q + part] = jnp.where(core == 0, both[1], both[0]).astype(BF16)
        pair_copy(q).start()

    def one_chunk(c, carry):
        edges_and_back(c)
        return carry

    def quarter(q, carry):
        lax.fori_loop(3 * q, 3 * q + 3, one_chunk, 0)
        finish(q)
        return carry

    lax.fori_loop(0, 4, quarter, 0)
    pair_copies = [pair_copy(q) for q in range(4)]

    place, second = y * other + x * core, x * other + y * core

    def attended_grad(j, carry):
        go[own, pl.ds(pl.multiple_of(128 + j * 256, 128), 256)] = (
            valid * dot(dres_v[0:T, :], w_v[lanes(j, 256), :], 1, 1)
        ).astype(BF16)
        return carry

    lax.fori_loop(0, W // 256, attended_grad, 0)
    wait(pair_copies)

    def pair_sum(a):
        blocks = [(a * other + b * core) * 4 + b * other + a * core for b in range(4)]
        mine = jnp.concatenate([lhs_own[block] for block in blocks], axis=0)
        theirs = jnp.concatenate([lhs_in[block] for block in blocks], axis=0)
        return dot(mine, att_v[...], 1, 0) + dot(theirs, att_m[...], 1, 0)

    half = 96
    whole = pair_sum((place + 2) % 4)
    s_2hop[0:half] = whole[0:half].astype(BF16)
    s_2hop[half:T] = whole[half:T].astype(BF16)
    two_hop = start([
        far(s_2hop.at[0:half], r_2hop.at[0:half], 1, up),
        far(s_2hop.at[half:T], r_2hop.at[half:T], 2, down),
    ])
    deltas = jnp.zeros((T, 128), F32)
    for head in range(H):
        start_, width = WINDOWS[head % 4]
        first = head // 4 * GROUP + start_
        product = (
            go[own, 128 + first : 128 + first + width].astype(F32)
            * att_v[0:T, first : first + width].astype(F32)
        )
        delta = jnp.sum(product * window_mask(head % 4), axis=1, keepdims=True)
        coarse = delta.astype(BF16).astype(F32)
        deltas = jnp.where(lane == head, coarse, deltas)
        deltas = jnp.where(lane == H + head, delta - coarse, deltas)
    go[own, 0:128] = deltas.astype(BF16)
    first, last = slice(0, 128 + GROUP), slice(128 + GROUP, 128 + W)

    def send_grads(cols, i):
        return start([
            near(go.at[own, cols], go.at[low, cols], i, right),
            near(go.at[own, cols], go.at[high, cols], i + 1, left),
        ])

    grad_copies = [send_grads(first, 18)]

    whole = pair_sum((place + 1) % 4)
    keep_up[...] = whole[0:half]
    s_up[half:T] = whole[half:T].astype(BF16)
    one_hop = start([far(s_up.at[half:T], r_up.at[half:T], 3, up)])
    whole = pair_sum((place + 3) % 4)
    s_down[0:half] = whole[0:half].astype(BF16)
    keep_down[...] = whole[half:T]
    one_hop += start([far(s_down.at[0:half], r_down.at[0:half], 4, down)])
    own_1[...] = pair_sum(place)

    def query_group(group):
        base = group * GROUP
        d_q = []
        for i in range(4):
            head = group * 4 + i
            start_, width = WINDOWS[i]
            cols = slice(base + start_, base + start_ + width)
            v_cols = slice(W + base + start_, W + base + start_ + width)
            g_cols = slice(128 + base + start_, 128 + base + start_ + width)
            g_head = go[own, g_cols] * window_mask(i).astype(BF16)
            delta = go[own, head : head + 1].astype(F32) + go[own, H + head : H + head + 1].astype(F32)
            slopes = dot(g_head, kv[:, v_cols], 1, 1)
            dscore = (probs[head].astype(F32) * ((slopes - delta) * SCALE)).astype(BF16)
            d_q.append(dot(dscore, kv[:, cols], 1, 0))
        out_v[:, base : base + GROUP] = join_heads(d_q).astype(BF16)

    def probs_group(group):
        base = group * GROUP
        for i in range(4):
            head = group * 4 + i
            start_, width = WINDOWS[i]
            cols = slice(base + start_, base + start_ + width)
            k_head = kv[own, cols] * window_mask(i).astype(BF16)
            scores = dot(q_all[:, cols], k_head, 1, 1)
            scores = jnp.where(pair_open, scores * (SCALE * LOG2E), NEG_FILL)
            probs_k[head] = jnp.exp2(scores - stat[:, head : head + 1]).astype(BF16)

    def key_group(group):
        base = group * GROUP
        d_k, d_v = [], []
        for i in range(4):
            head = group * 4 + i
            start_, width = WINDOWS[i]
            cols = slice(base + start_, base + start_ + width)
            v_cols = slice(W + base + start_, W + base + start_ + width)
            g_win = go[:, 128 + base + start_ : 128 + base + start_ + width]
            v_head = kv[own, v_cols] * window_mask(i).astype(BF16)
            delta = go[:, head : head + 1].astype(F32) + go[:, H + head : H + head + 1].astype(F32)
            slopes = dot(g_win, v_head, 1, 1)
            weights = probs_k[head]
            dscore = (weights.astype(F32) * ((slopes - delta) * SCALE)).astype(BF16)
            d_k.append(dot(dscore, q_all[:, cols], 0, 0))
            d_v.append(dot(weights, g_win, 0, 0))
        out_v[:, W + base : W + base + GROUP] = join_heads(d_k).astype(BF16)
        out_v[:, 2 * W + base : 2 * W + base + GROUP] = join_heads(d_v).astype(BF16)

    query_group(0)
    wait(two_hop)
    s_up[0:half] = (keep_up[...] + r_2hop[0:half].astype(F32)).astype(BF16)
    one_hop += start([far(s_up.at[0:half], r_up.at[0:half], 5, up)])
    s_down[half:T] = (keep_down[...] + r_2hop[half:T].astype(F32)).astype(BF16)
    one_hop += start([far(s_down.at[half:T], r_down.at[half:T], 6, down)])

    query_group(1)
    wait(q_copies)
    probs_group(0)
    probs_group(1)

    wait(one_hop)
    grad_copies.append(send_grads(last, 20))
    second_copies = []
    for s in (1, 0, 2, 3):
        rows = pl.ds(pl.multiple_of((second + 1 + s) % 4 * 48, 16), 48)
        total = own_1[rows, :] + r_up[rows, :].astype(F32) + r_down[rows, :].astype(F32)
        if s < 3:
            s_2[s] = total.astype(BF16)
            second_copies += start([far(s_2.at[s], r_2.at[s], 7 + s, second_peers[s])])
        else:
            own_2[...] = total

    wait(grad_copies[0])
    key_group(0)

    wait(second_copies)
    total = own_2[...]
    for e in range(3):
        total = total + r_2[e].astype(F32)
    for part in range(8):
        s_3[part, 0:6, :] = total[part * 6 : part * 6 + 6]
    z_copies = []
    for e in (3, 2, 4, 1, 5, 0, 6):
        peer, part = z_peers[e]
        z_copies += start([far(s_3.at[part], r_3.at[e], 19 + e, peer)])

    wait(grad_copies[1])
    key_group(1)

    wait(z_copies)
    total = s_3[zl * 4 + zh]
    for e in range(7):
        total = total + r_3[e]
    sums_o[...] = total


def hand_over(dres_i, dqkv_i, sums_i, dres_o, dqkv_o, dproj_o, dker_o, proj_v, ker_v, sem):
    copies = [
        pltpu.make_async_copy(dqkv_i, dqkv_o.at[0], sem.at[0]),
        pltpu.make_async_copy(dres_i.at[0:T], dres_o.at[0], sem.at[1]),
        pltpu.make_async_copy(proj_v, dproj_o, sem.at[2]),
        pltpu.make_async_copy(ker_v, dker_o, sem.at[3]),
    ]
    copies[0].start()
    copies[1].start()
    proj_v[...] = sums_i[0:6, 0:W]
    copies[2].start()
    ker_v[...] = sums_i[0:6, W : W + TAPS]
    copies[3].start()
    for copy in copies:
        copy.wait()


def local(resid, qkv, cotangent, lengths, out_proj, ker):
    hbm = pl.BlockSpec(memory_space=pl.ANY)
    vmem = pl.BlockSpec(memory_space=pltpu.VMEM)
    scratch = [
        ((KEYS, W), BF16), ((KEYS, 2 * W), BF16), ((T, D), BF16), ((T, D), BF16),
        ((W, D), BF16), ((TAPS, D), F32), ((H, T, KEYS), BF16), ((H, KEYS, T), BF16),
        ((KEYS, 128), F32), ((256, RW), BF16), ((256, RW), BF16), ((KEYS, RW), BF16),
        ((CHUNKS, T + 2 * REACH, 128), F32), ((CHUNKS, T + 2 * EDGE, 128), F32),
        ((2, REACH, D), BF16), ((2, REACH, D), BF16), ((2, EDGE, D), BF16), ((T, D), F32),
        ((CHUNKS, 8 * TAPS, 128), F32),
        ((16, 48, 256), BF16), ((16, 48, 256), BF16), ((16, 48, 256), BF16),
        ((T, RW), BF16), ((T, RW), BF16), ((T, RW), BF16), ((T, RW), BF16),
        ((T // 2, RW), F32), ((T // 2, RW), F32), ((T, RW), BF16), ((T, RW), BF16),
        ((T, RW), F32),
        ((3, 48, RW), BF16), ((3, 48, RW), BF16), ((48, RW), F32),
        ((8, 8, RW), F32), ((7, 8, RW), F32),
    ]
    dres, dqkv, sums = pl.pallas_call(
        kernel,
        out_shape=[
            pltpu.VMEM((256, D), BF16),
            pltpu.VMEM((T, 3 * W), BF16),
            pltpu.VMEM((8, RW), F32),
        ],
        in_specs=[hbm, hbm, hbm, pl.BlockSpec(memory_space=pltpu.SMEM), hbm, hbm],
        out_specs=[vmem, vmem, vmem],
        scratch_shapes=[pltpu.VMEM(shape, kind) for shape, kind in scratch]
        + [
            pltpu.SemaphoreType.DMA((8,)),
            pltpu.SemaphoreType.DMA((22,)),
            pltpu.SemaphoreType.DMA((22,)),
            pltpu.SemaphoreType.DMA((26,)),
            pltpu.SemaphoreType.DMA((26,)),
        ],
        compiler_params=pltpu.CompilerParams(
            collective_id=0, has_side_effects=True, vmem_limit_bytes=60 * 2**20
        ),
        cost_estimate=pl.CostEstimate(
            flops=3_000_000_000, bytes_accessed=8_000_000, transcendentals=1_000_000
        ),
    )(resid, qkv, cotangent, lengths, out_proj, ker)
    dres, dqkv, dproj, dker = pl.pallas_call(
        hand_over,
        out_shape=[
            jax.ShapeDtypeStruct((1, T, D), BF16),
            jax.ShapeDtypeStruct((1, T, 3 * W), BF16),
            jax.ShapeDtypeStruct((6, W), F32),
            jax.ShapeDtypeStruct((6, TAPS), F32),
        ],
        in_specs=[vmem, vmem, vmem],
        out_specs=[hbm, hbm, hbm, hbm],
        scratch_shapes=[
            pltpu.VMEM((6, W), F32),
            pltpu.VMEM((6, TAPS), F32),
            pltpu.SemaphoreType.DMA((4,)),
        ],
        compiler_params=pltpu.CompilerParams(vmem_limit_bytes=8 * 2**20),
        cost_estimate=pl.CostEstimate(flops=0, bytes_accessed=4_000_000, transcendentals=0),
    )(dres, dqkv, sums)
    return dres, dqkv, dproj.T, dker.T


def solution(mesh):
    in_specs = (P("dp", "tm", None), P("dp", "tm", None), P("dp", "tm", None), P("dp"), P(), P())
    out_specs = (
        P("dp", "tm", None),
        P("dp", "tm", None),
        P(None, ("tm", "dp")),
        P(None, ("tm", "dp")),
    )
    return jax.shard_map(local, mesh=mesh, in_specs=in_specs, out_specs=out_specs, check_vma=False)
```

```python
import jax
import jax.numpy as jnp
from jax import lax
from jax.experimental import pallas as pl
from jax.experimental.pallas import tpu as pltpu
from jax.sharding import PartitionSpec as P

H = 8
HD = 96
T = 192
D = 1536
W = 768
TAPS = 31
CHUNKS = D // 128
EDGE = 16
REACH = 2 * EDGE
RW = W + 128
KEYS = 3 * T
GROUP = 4 * HD
WINDOWS = ((0, 128), (0, 256), (128, 256), (256, 128))
NEG_FILL = -1000000000.0
SCALE = HD ** (-0.5)
LOG2E = 1.4426950408889634
MESH = pl.DeviceIdType.MESH
F32 = jnp.float32
BF16 = jnp.bfloat16


def dot(a, b, ca, cb):
    return lax.dot_general(a, b, (((ca,), (cb,)), ((), ())), preferred_element_type=F32)


def window_mask(i):
    start, width = WINDOWS[i]
    lane = lax.broadcasted_iota(jnp.int32, (1, width), 1) + start
    return ((lane >= i * HD) & (lane < (i + 1) * HD)).astype(F32)


def join_heads(parts):
    lane = lax.broadcasted_iota(jnp.int32, (1, 128), 1)
    first = jnp.where(lane < 96, parts[0], parts[1][:, :128])
    second = jnp.where(lane < 64, parts[1][:, 128:], parts[2][:, :128])
    third = jnp.where(lane < 32, parts[2][:, 128:], parts[3])
    return jnp.concatenate([first, second, third], axis=1)


def lanes(c, width):
    return pl.ds(pl.multiple_of(c * width, width), width)


def kernel(
    resid_h, qkv_h, cot_h, len_s, proj_h, ker_h,
    dres_v, out_v, sums_o,
    q_all, kv, res_v, cot_v, w_v, ker_v, probs, probs_k, stat, att_v, att_m, go,
    mext, gext, hs, hm, hc, mix, kt_part, lhs_own, lhs_out, lhs_in,
    s_2hop, r_2hop, s_up, s_down, keep_up, keep_down, r_up, r_down, own_1,
    s_2, r_2, own_2, s_3, r_3,
    loc_sem, nb_send, nb_recv, rs_send, rs_recv,
):
    tm = lax.axis_index("tm")
    zh = lax.axis_index("dp")
    core = tm % 2
    zl = (tm // 2) % 2
    x = (tm // 4) % 4
    y = tm // 16
    other = 1 - core
    zz = zh * 2 + zl

    def device(y_, x_, zl_, core_, zh_):
        return {"tm": ((y_ * 4 + x_) * 2 + zl_) * 2 + core_, "dp": zh_}

    left = {"tm": (tm + 63) % 64, "dp": zh}
    right = {"tm": (tm + 1) % 64, "dp": zh}
    mate = device(y, x, zl, other, zh)
    up = device((y + other) % 4, (x + core) % 4, zl, core, zh)
    down = device((y + 3 * other) % 4, (x + 3 * core) % 4, zl, core, zh)
    second_peers = [device((y + e * core) % 4, (x + e * other) % 4, zl, core, zh) for e in (1, 2, 3)]
    z_peers = []
    for e in range(1, 8):
        z_to = (zz + e) % 8
        z_peers.append((device(y, x, z_to % 2, core, z_to // 2), (z_to % 2) * 4 + z_to // 2))

    def local(src, dst, i):
        return pltpu.make_async_copy(src, dst, loc_sem.at[i])

    def near(src, dst, i, to):
        return pltpu.make_async_remote_copy(
            src_ref=src, dst_ref=dst, send_sem=nb_send.at[i], recv_sem=nb_recv.at[i],
            device_id=to, device_id_type=MESH,
        )

    def far(src, dst, i, to):
        return pltpu.make_async_remote_copy(
            src_ref=src, dst_ref=dst, send_sem=rs_send.at[i], recv_sem=rs_recv.at[i],
            device_id=to, device_id_type=MESH,
        )

    def start(copies):
        for copy in copies:
            copy.start()
        return copies

    def wait(copies):
        for copy in copies:
            copy.wait()

    low, own, high = slice(0, T), slice(T, 2 * T), slice(2 * T, 3 * T)

    ins = start([
        local(qkv_h.at[0, :, 0:W], q_all.at[own], 0),
        local(qkv_h.at[0, :, W : 3 * W], kv.at[own], 1),
        local(proj_h, w_v, 2),
        local(resid_h.at[0], res_v, 3),
        local(cot_h.at[0], cot_v, 4),
        local(ker_h, ker_v, 5),
    ])

    barrier = pltpu.get_barrier_semaphore()
    everyone = [left, right, up, down] + second_peers + [peer for peer, _ in z_peers]
    for peer in everyone:
        pl.semaphore_signal(barrier, inc=1, device_id=peer, device_id_type=MESH)

    pl.semaphore_wait(barrier, len(everyone))

    kv_copies = []
    for group in range(2):
        for part in range(2):
            cols = slice(part * W + group * GROUP, part * W + (group + 1) * GROUP)
            src = qkv_h.at[0, :, W + cols.start : W + cols.stop]
            i = group * 4 + part * 2
            kv_copies.append(near(src, kv.at[low, cols], i, right))
            kv_copies.append(near(src, kv.at[high, cols], i + 1, left))
    start(kv_copies)

    length = len_s[0]
    first_frame = tm * T
    frame = first_frame + lax.broadcasted_iota(jnp.int32, (T, 1), 0)
    valid = (frame < length).astype(F32)
    key = first_frame - T + lax.broadcasted_iota(jnp.int32, (1, KEYS), 1)
    key_open = (key >= 0) & (key < length)
    own_key = first_frame + lax.broadcasted_iota(jnp.int32, (1, T), 1)
    near_query = first_frame - T + lax.broadcasted_iota(jnp.int32, (KEYS, 1), 0)
    pair_open = (own_key < length) & (near_query >= 0) & (near_query < 64 * T)
    has_left = (tm > 0).astype(F32)
    has_right = (tm < 63).astype(F32)
    lane = lax.broadcasted_iota(jnp.int32, (1, 128), 1)

    eye_row = lax.broadcasted_iota(jnp.int32, (256 - T, 128), 0)
    eye_col = lax.broadcasted_iota(jnp.int32, (256 - T, 128), 1)
    att_v[T:256, 0:W] = jnp.zeros((256 - T, W), BF16)
    att_v[0:T, W:RW] = jnp.zeros((T, 128), BF16)
    att_v[T:256, W:RW] = ((eye_row == eye_col) & (eye_row < 32)).astype(F32).astype(BF16)
    dres_v[T:256, :] = jnp.zeros((256 - T, D), BF16)
    s_3[...] = jnp.zeros_like(s_3)

    wait(ins)
    wait(kv_copies[:4])

    def forward_group(group, stats):
        base = group * GROUP
        outs = []
        for i in range(4):
            start_, width = WINDOWS[i]
            cols = slice(base + start_, base + start_ + width)
            v_cols = slice(W + base + start_, W + base + start_ + width)
            q_head = q_all[own, cols] * window_mask(i).astype(BF16)
            scores = dot(q_head, kv[:, cols], 1, 1)
            scores = jnp.where(key_open, scores * (SCALE * LOG2E), NEG_FILL)
            peak = jnp.max(scores, axis=1, keepdims=True)
            weights = jnp.exp2(scores - peak)
            total = jnp.sum(weights, axis=1, keepdims=True)
            weights = (weights * (1.0 / total)).astype(BF16)
            probs[group * 4 + i] = weights
            stats = jnp.where(lane == group * 4 + i, peak + jnp.log2(total), stats)
            outs.append(dot(weights, kv[:, v_cols], 1, 0))
        att_v[0:T, base : base + GROUP] = (join_heads(outs) * valid).astype(BF16)
        return stats

    def project_half(j, carry):
        cols = lanes(j, 256)
        mix[:, cols] = res_v[:, cols].astype(F32) + dot(
            att_v[0:T, 0:GROUP], w_v[0:GROUP, cols], 1, 0
        )
        return carry

    stats = forward_group(0, jnp.zeros((T, 128), F32))
    lax.fori_loop(0, D // 256, project_half, 0)
    wait(kv_copies[4:])
    early = start([
        near(cot_v.at[0:EDGE], hc.at[1], 8, left),
        near(cot_v.at[T - EDGE : T], hc.at[0], 9, right),
    ])
    q_copies = start([
        near(q_all.at[own, 0:GROUP], q_all.at[low, 0:GROUP], 10, right),
        near(q_all.at[own, 0:GROUP], q_all.at[high, 0:GROUP], 11, left),
    ])
    stat[own, :] = forward_group(1, stats)
    early += start([far(att_v, att_m, 0, mate)])

    def project(j, carry):
        cols = lanes(j, 256)
        mixed = mix[:, cols] + dot(att_v[0:T, GROUP:W], w_v[GROUP:W, cols], 1, 0)
        masked = (mixed.astype(BF16).astype(F32) * valid).astype(BF16)
        hs[0, :, cols] = masked[0:REACH]
        hs[1, :, cols] = masked[T - REACH : T]
        wide = masked.astype(F32)
        mext[2 * j, REACH : REACH + T, :] = wide[:, :128]
        mext[2 * j + 1, REACH : REACH + T, :] = wide[:, 128:]
        return carry

    lax.fori_loop(0, D // 256, project, 0)
    mask_halo = start([near(hs.at[0], hm.at[1], 12, left), near(hs.at[1], hm.at[0], 13, right)])

    def windows(src, c, first, count):
        for s in range(8):
            taps = range(s, TAPS, 8)
            window = src[c, first + s : first + s + count + 8 * (len(taps) - 1), :]
            for place, j in enumerate(taps):
                yield j, window[8 * place : 8 * place + count]

    def convolve(src, c, first, count, flip):
        total = None
        for j, rows in windows(src, c, first, count):
            tap = TAPS - 1 - j if flip else j
            term = ker_v[tap : tap + 1, lanes(c, 128)] * rows
            total = term if total is None else total + term
        return total

    def conv_rows(c, row, count, cot):
        conv = convolve(mext, c, row + REACH - 15, count, False)
        sigma = jax.nn.sigmoid(conv)
        slope = sigma * (1.0 + conv * (1.0 - sigma))
        grad = (cot * slope).astype(BF16).astype(F32)
        gext[c, EDGE + row : EDGE + row + count, :] = grad

    def back_rows(c, row, count):
        cols = lanes(c, 128)
        back = convolve(gext, c, row + EDGE - 15, count, True)
        cot = cot_v[row : row + count, cols].astype(F32)
        dres_v[row : row + count, cols] = (cot + valid[row : row + count] * back).astype(BF16)

    def kernel_terms(c, row, count, sums):
        grad = gext[c, EDGE + row : EDGE + row + count, :]
        for j, rows in windows(mext, c, row + REACH - 15, count):
            term = jnp.sum((grad * rows).reshape(count // 8, 8, 128), axis=0)
            sums[j] = term if sums[j] is None else sums[j] + term

    def conv_inner(c, carry):
        for row in (16, 96):
            conv_rows(c, row, 80, cot_v[row : row + 80, lanes(c, 128)].astype(F32))
        sums = [None] * TAPS
        for row in (16, 96):
            kernel_terms(c, row, 80, sums)
        for j in range(TAPS):
            kt_part[c, 8 * j : 8 * j + 8, :] = sums[j]
        back_rows(c, 32, 64)
        back_rows(c, 96, 64)
        return carry

    lax.fori_loop(0, CHUNKS // 2, conv_inner, 0)
    q_copies += start([
        near(q_all.at[own, GROUP:W], q_all.at[low, GROUP:W], 14, right),
        near(q_all.at[own, GROUP:W], q_all.at[high, GROUP:W], 15, left),
        near(stat.at[own], stat.at[low], 16, right),
        near(stat.at[own], stat.at[high], 17, left),
    ])
    lax.fori_loop(CHUNKS // 2, CHUNKS, conv_inner, 0)
    wait(early)
    wait(mask_halo)

    def edges_and_back(c):
        cols = lanes(c, 128)
        mext[c, 0:REACH, :] = hm[0, :, cols].astype(F32) * has_left
        mext[c, REACH + T : 2 * REACH + T, :] = hm[1, :, cols].astype(F32) * has_right
        cot = cot_v[0:EDGE, cols].astype(F32)
        before = hc[0, :, cols].astype(F32) * has_left
        conv_rows(c, -EDGE, REACH, jnp.concatenate([before, cot], axis=0))
        cot = cot_v[T - EDGE : T, cols].astype(F32)
        after = hc[1, :, cols].astype(F32) * has_right
        conv_rows(c, T - EDGE, REACH, jnp.concatenate([cot, after], axis=0))
        sums = [kt_part[c, 8 * j : 8 * j + 8, :] for j in range(TAPS)]
        kernel_terms(c, 0, EDGE, sums)
        kernel_terms(c, T - EDGE, EDGE, sums)
        for j in range(TAPS):
            kt_part[c, 8 * j : 8 * j + 8, :] = sums[j]
        back_rows(c, 0, 32)
        back_rows(c, T - 32, 32)

    tap_row = lax.broadcasted_iota(jnp.int32, (32, 8 * TAPS), 0)
    tap_col = lax.broadcasted_iota(jnp.int32, (32, 8 * TAPS), 1)
    adder = (tap_col // 8 == tap_row).astype(F32).astype(BF16)

    def pair_copy(q):
        quarter = pl.ds(4 * q, 4)
        return far(lhs_out.at[quarter], lhs_in.at[quarter], 15 + q, mate)

    def finish(q):
        cols = lanes(q, 384)
        terms = jnp.concatenate([kt_part[3 * q + i].astype(BF16) for i in range(3)], axis=1)
        dres_v[T : T + 32, cols] = dot(adder, terms, 1, 0).astype(BF16)
        turned = dres_v[:, cols].T.astype(F32)
        for part in range(4):
            row = 96 * part
            both = [
                jnp.concatenate(
                    [turned[row + 24 * i : row + 24 * i + 24], turned[row + 48 + 24 * i : row + 72 + 24 * i]],
                    axis=0,
                )
                for i in range(2)
            ]
            lhs_own[4 * q + part] = jnp.where(core == 0, both[0], both[1]).astype(BF16)
            lhs_out[4 * q + part] = jnp.where(core == 0, both[1], both[0]).astype(BF16)
        pair_copy(q).start()

    def one_chunk(c, carry):
        edges_and_back(c)
        return carry

    def quarter(q, carry):
        lax.fori_loop(3 * q, 3 * q + 3, one_chunk, 0)
        finish(q)
        return carry

    lax.fori_loop(0, 4, quarter, 0)
    pair_copies = [pair_copy(q) for q in range(4)]

    place, second = y * other + x * core, x * other + y * core

    def attended_grad(j, carry):
        go[own, pl.ds(pl.multiple_of(128 + j * 256, 128), 256)] = (
            valid * dot(dres_v[0:T, :], w_v[lanes(j, 256), :], 1, 1)
        ).astype(BF16)
        return carry

    lax.fori_loop(0, W // 256, attended_grad, 0)
    wait(pair_copies)

    def pair_sum(a):
        blocks = [(a * other + b * core) * 4 + b * other + a * core for b in range(4)]
        mine = jnp.concatenate([lhs_own[block] for block in blocks], axis=0)
        theirs = jnp.concatenate([lhs_in[block] for block in blocks], axis=0)
        return dot(mine, att_v[...], 1, 0) + dot(theirs, att_m[...], 1, 0)

    half = 96
    whole = pair_sum((place + 2) % 4)
    s_2hop[0:half] = whole[0:half].astype(BF16)
    s_2hop[half:T] = whole[half:T].astype(BF16)
    two_hop = start([
        far(s_2hop.at[0:half], r_2hop.at[0:half], 1, up),
        far(s_2hop.at[half:T], r_2hop.at[half:T], 2, down),
    ])
    deltas = jnp.zeros((T, 128), F32)
    for head in range(H):
        start_, width = WINDOWS[head % 4]
        first = head // 4 * GROUP + start_
        product = (
            go[own, 128 + first : 128 + first + width].astype(F32)
            * att_v[0:T, first : first + width].astype(F32)
        )
        delta = jnp.sum(product * window_mask(head % 4), axis=1, keepdims=True)
        coarse = delta.astype(BF16).astype(F32)
        deltas = jnp.where(lane == head, coarse, deltas)
        deltas = jnp.where(lane == H + head, delta - coarse, deltas)
    go[own, 0:128] = deltas.astype(BF16)
    first, last = slice(0, 128 + GROUP), slice(128 + GROUP, 128 + W)

    def send_grads(cols, i):
        return start([
            near(go.at[own, cols], go.at[low, cols], i, right),
            near(go.at[own, cols], go.at[high, cols], i + 1, left),
        ])

    grad_copies = [send_grads(first, 18)]

    whole = pair_sum((place + 1) % 4)
    keep_up[...] = whole[0:half]
    s_up[half:T] = whole[half:T].astype(BF16)
    one_hop = start([far(s_up.at[half:T], r_up.at[half:T], 3, up)])
    whole = pair_sum((place + 3) % 4)
    s_down[0:half] = whole[0:half].astype(BF16)
    keep_down[...] = whole[half:T]
    one_hop += start([far(s_down.at[0:half], r_down.at[0:half], 4, down)])
    own_1[...] = pair_sum(place)

    def query_group(group):
        base = group * GROUP
        d_q = []
        for i in range(4):
            head = group * 4 + i
            start_, width = WINDOWS[i]
            cols = slice(base + start_, base + start_ + width)
            v_cols = slice(W + base + start_, W + base + start_ + width)
            g_cols = slice(128 + base + start_, 128 + base + start_ + width)
            g_head = go[own, g_cols] * window_mask(i).astype(BF16)
            delta = go[own, head : head + 1].astype(F32) + go[own, H + head : H + head + 1].astype(F32)
            slopes = dot(g_head, kv[:, v_cols], 1, 1)
            dscore = (probs[head].astype(F32) * ((slopes - delta) * SCALE)).astype(BF16)
            d_q.append(dot(dscore, kv[:, cols], 1, 0))
        out_v[:, base : base + GROUP] = join_heads(d_q).astype(BF16)

    def probs_group(group):
        base = group * GROUP
        for i in range(4):
            head = group * 4 + i
            start_, width = WINDOWS[i]
            cols = slice(base + start_, base + start_ + width)
            k_head = kv[own, cols] * window_mask(i).astype(BF16)
            scores = dot(q_all[:, cols], k_head, 1, 1)
            scores = jnp.where(pair_open, scores * (SCALE * LOG2E), NEG_FILL)
            probs_k[head] = jnp.exp2(scores - stat[:, head : head + 1]).astype(BF16)

    def key_group(group):
        base = group * GROUP
        d_k, d_v = [], []
        for i in range(4):
            head = group * 4 + i
            start_, width = WINDOWS[i]
            cols = slice(base + start_, base + start_ + width)
            v_cols = slice(W + base + start_, W + base + start_ + width)
            g_win = go[:, 128 + base + start_ : 128 + base + start_ + width]
            v_head = kv[own, v_cols] * window_mask(i).astype(BF16)
            delta = go[:, head : head + 1].astype(F32) + go[:, H + head : H + head + 1].astype(F32)
            slopes = dot(g_win, v_head, 1, 1)
            weights = probs_k[head]
            dscore = (weights.astype(F32) * ((slopes - delta) * SCALE)).astype(BF16)
            d_k.append(dot(dscore, q_all[:, cols], 0, 0))
            d_v.append(dot(weights, g_win, 0, 0))
        out_v[:, W + base : W + base + GROUP] = join_heads(d_k).astype(BF16)
        out_v[:, 2 * W + base : 2 * W + base + GROUP] = join_heads(d_v).astype(BF16)

    query_group(0)
    wait(two_hop)
    s_up[0:half] = (keep_up[...] + r_2hop[0:half].astype(F32)).astype(BF16)
    one_hop += start([far(s_up.at[0:half], r_up.at[0:half], 5, up)])
    s_down[half:T] = (keep_down[...] + r_2hop[half:T].astype(F32)).astype(BF16)
    one_hop += start([far(s_down.at[half:T], r_down.at[half:T], 6, down)])

    query_group(1)
    wait(q_copies)
    probs_group(0)
    probs_group(1)

    wait(one_hop)
    second_copies = []
    for s in (1, 0, 2, 3):
        rows = pl.ds(pl.multiple_of((second + 1 + s) % 4 * 48, 16), 48)
        total = own_1[rows, :] + r_up[rows, :].astype(F32) + r_down[rows, :].astype(F32)
        if s < 3:
            s_2[s] = total.astype(BF16)
            second_copies += start([far(s_2.at[s], r_2.at[s], 7 + s, second_peers[s])])
        else:
            own_2[...] = total
    grad_copies.append(send_grads(last, 20))

    wait(grad_copies[0])
    key_group(0)

    wait(second_copies)
    total = own_2[...]
    for e in range(3):
        total = total + r_2[e].astype(F32)
    for part in range(8):
        s_3[part, 0:6, :] = total[part * 6 : part * 6 + 6]
    z_copies = []
    for e in (3, 2, 4, 1, 5, 0, 6):
        peer, part = z_peers[e]
        z_copies += start([far(s_3.at[part], r_3.at[e], 19 + e, peer)])

    wait(grad_copies[1])
    key_group(1)

    wait(z_copies)
    total = s_3[zl * 4 + zh]
    for e in range(7):
        total = total + r_3[e]
    sums_o[...] = total


def hand_over(dres_i, dqkv_i, sums_i, dres_o, dqkv_o, dproj_o, dker_o, proj_v, ker_v, sem):
    copies = [
        pltpu.make_async_copy(dqkv_i, dqkv_o.at[0], sem.at[0]),
        pltpu.make_async_copy(dres_i.at[0:T], dres_o.at[0], sem.at[1]),
        pltpu.make_async_copy(proj_v, dproj_o, sem.at[2]),
        pltpu.make_async_copy(ker_v, dker_o, sem.at[3]),
    ]
    copies[0].start()
    copies[1].start()
    proj_v[...] = sums_i[0:6, 0:W]
    copies[2].start()
    ker_v[...] = sums_i[0:6, W : W + TAPS]
    copies[3].start()
    for copy in copies:
        copy.wait()


def local(resid, qkv, cotangent, lengths, out_proj, ker):
    hbm = pl.BlockSpec(memory_space=pl.ANY)
    vmem = pl.BlockSpec(memory_space=pltpu.VMEM)
    scratch = [
        ((KEYS, W), BF16), ((KEYS, 2 * W), BF16), ((T, D), BF16), ((T, D), BF16),
        ((W, D), BF16), ((TAPS, D), F32), ((H, T, KEYS), BF16), ((H, KEYS, T), BF16),
        ((KEYS, 128), F32), ((256, RW), BF16), ((256, RW), BF16), ((KEYS, RW), BF16),
        ((CHUNKS, T + 2 * REACH, 128), F32), ((CHUNKS, T + 2 * EDGE, 128), F32),
        ((2, REACH, D), BF16), ((2, REACH, D), BF16), ((2, EDGE, D), BF16), ((T, D), F32),
        ((CHUNKS, 8 * TAPS, 128), F32),
        ((16, 48, 256), BF16), ((16, 48, 256), BF16), ((16, 48, 256), BF16),
        ((T, RW), BF16), ((T, RW), BF16), ((T, RW), BF16), ((T, RW), BF16),
        ((T // 2, RW), F32), ((T // 2, RW), F32), ((T, RW), BF16), ((T, RW), BF16),
        ((T, RW), F32),
        ((3, 48, RW), BF16), ((3, 48, RW), BF16), ((48, RW), F32),
        ((8, 8, RW), F32), ((7, 8, RW), F32),
    ]
    dres, dqkv, sums = pl.pallas_call(
        kernel,
        out_shape=[
            pltpu.VMEM((256, D), BF16),
            pltpu.VMEM((T, 3 * W), BF16),
            pltpu.VMEM((8, RW), F32),
        ],
        in_specs=[hbm, hbm, hbm, pl.BlockSpec(memory_space=pltpu.SMEM), hbm, hbm],
        out_specs=[vmem, vmem, vmem],
        scratch_shapes=[pltpu.VMEM(shape, kind) for shape, kind in scratch]
        + [
            pltpu.SemaphoreType.DMA((8,)),
            pltpu.SemaphoreType.DMA((22,)),
            pltpu.SemaphoreType.DMA((22,)),
            pltpu.SemaphoreType.DMA((26,)),
            pltpu.SemaphoreType.DMA((26,)),
        ],
        compiler_params=pltpu.CompilerParams(
            collective_id=0, has_side_effects=True, vmem_limit_bytes=60 * 2**20
        ),
        cost_estimate=pl.CostEstimate(
            flops=3_000_000_000, bytes_accessed=8_000_000, transcendentals=1_000_000
        ),
    )(resid, qkv, cotangent, lengths, out_proj, ker)
    dres, dqkv, dproj, dker = pl.pallas_call(
        hand_over,
        out_shape=[
            jax.ShapeDtypeStruct((1, T, D), BF16),
            jax.ShapeDtypeStruct((1, T, 3 * W), BF16),
            jax.ShapeDtypeStruct((6, W), F32),
            jax.ShapeDtypeStruct((6, TAPS), F32),
        ],
        in_specs=[vmem, vmem, vmem],
        out_specs=[hbm, hbm, hbm, hbm],
        scratch_shapes=[
            pltpu.VMEM((6, W), F32),
            pltpu.VMEM((6, TAPS), F32),
            pltpu.SemaphoreType.DMA((4,)),
        ],
        compiler_params=pltpu.CompilerParams(vmem_limit_bytes=8 * 2**20),
        cost_estimate=pl.CostEstimate(flops=0, bytes_accessed=4_000_000, transcendentals=0),
    )(dres, dqkv, sums)
    return dres, dqkv, dproj.T, dker.T


def solution(mesh):
    in_specs = (P("dp", "tm", None), P("dp", "tm", None), P("dp", "tm", None), P("dp"), P(), P())
    out_specs = (
        P("dp", "tm", None),
        P("dp", "tm", None),
        P(None, ("tm", "dp")),
        P(None, ("tm", "dp")),
    )
    return jax.shard_map(local, mesh=mesh, in_specs=in_specs, out_specs=out_specs, check_vma=False)
```
